256 devices in a mesh: gx: 32 (over z, y), gy: 2 (over core), gz: 4 (over x).
Axes of the slice: x: 4, y: 4, z: 8, core: 2. Of those that a mesh axis runs over, the one named last changes fastest.
Arguments:
- source: float32 [4, 4, 4, 128, 8, 512], P(None, None, None, 'gx', 'gy', 'gz'), may hold values from -6 to 6
- coefficient: float32 [128, 8, 512], P('gx', 'gy', 'gz'), may hold values from 0.2 to 5
- orientation: int32 [6, 128, 8, 512], P(None, 'gx', 'gy', 'gz'), may hold values from 0 to 7
Outputs:
- solution: float32 [4, 4, 4, 128, 8, 512], P(None, None, None, 'gx', 'gy', 'gz')
The draws below stay inside these ranges and needn't reach their ends.
All inputs are finite; a program needn't handle non-finite values.
Results may differ from the reference program's by a relative error of at most 0.0001.
Values sent between devices are 32-bit elements; how exact they have to be, the bound alone decides.
A program may use at most 128 MiB of HBM per device.

```python
import math
import jax
import jax.numpy as jnp
import numpy as np
from jax import lax

NODES = 4
LOC = 2
AGG = 2
NX = 128
NY = 8
NZ = 512


def touch_ends(values, stream_key, least, top_value):
    dims = values.shape
    spot = [jax.random.randint(jax.random.fold_in(stream_key, axis), (), 0, dims[axis]) for axis in range(len(dims))]
    values = values.at[tuple(spot)].set(least)
    longest = dims.index(max(dims))
    spot[longest] = (spot[longest] + 1) % dims[longest]
    return values.at[tuple(spot)].set(top_value)


def steps_of(own_key, extent, shards, least, high):
    gain = 1.0
    for position, shards_of in shards:
        heights = jax.random.uniform(jax.random.fold_in(jax.random.fold_in(own_key, 6), position), (shards_of,), jnp.float32, least / len(shards), high / len(shards))
        gain = gain * jnp.repeat(jnp.exp(heights), extent[position] // shards_of).reshape((-1,) + (1,) * (len(extent) - 1 - position))
    return gain


def gaussian(key, shape, deviation, most, cuts=(), kind=jnp.bfloat16):
    values = jax.random.normal(key, shape, jnp.float32) * deviation
    if len(cuts) > 0:
        values = steps_of(key, shape, cuts, -0.22, 0.18) * values
    return jnp.clip(values, min=-most, max=most).astype(kind)


def setup_inputs(seed: int = 0) -> dict:
    streams_of = jax.random.split(jax.random.key(seed), 4)
    return {
        "source": gaussian(streams_of[0], (NODES, NODES, NODES, NX, NY, NZ), 1.0, 6.0, ((3, 32), (4, 2), (5, 4)), jnp.float32),
        "coefficient": jnp.clip(jnp.exp(math.log(5.0) - 3.218876 * jax.random.uniform(streams_of[1], (NX, NY, NZ), jnp.float32) ** steps_of(streams_of[1], (NX, NY, NZ), ((0, 32), (1, 2), (2, 4)), -0.2, 0.2)), 0.2, 5.0),
        "orientation": touch_ends(jax.random.randint(streams_of[2], (6, NX, NY, NZ), 0, 8), jax.random.fold_in(streams_of[2], 1), 0, 7).astype(jnp.int32),
    }


EXACT = lax.Precision.HIGHEST
TAU = 6.0
SHIFT = 1.0
OMEGA = 0.8

def lagrange(points, node_points):
    table = np.ones((points.shape[0], 4))
    for column in range(4):
        for other in range(4):
            if other != column:
                table[:, column] *= (points - node_points[other]) / (node_points[column] - node_points[other])
    return table

def identity_four():
    table = np.zeros((4, 4))
    for index in range(4):
        table[index, index] = 1.0
    return table

def jacobi_eigen(matrix):
    current = matrix.copy()
    vectors = identity_four()
    for sweep in range(12):
        for first in range(3):
            for second in range(first + 1, 4):
                angle = 0.5 * math.atan2(2.0 * current[first, second], current[second, second] - current[first, first])
                cosine = math.cos(angle)
                sine = math.sin(angle)
                rotation = identity_four()
                rotation[first, first] = cosine
                rotation[second, second] = cosine
                rotation[first, second] = sine
                rotation[second, first] = -sine
                current = rotation.T @ current @ rotation
                vectors = vectors @ rotation
    values = np.array([current[index, index] for index in range(4)])
    return (values, vectors)

def tables():
    node_points = np.array([-1.0, -1.0 / math.sqrt(5.0), 1.0 / math.sqrt(5.0), 1.0])
    weights = np.array([1.0, 5.0, 5.0, 1.0]) / 6.0
    derivative = np.zeros((4, 4))
    for column in range(4):
        for other in range(4):
            if other != column:
                term = np.full(4, 1.0 / (node_points[column] - node_points[other]))
                for third in range(4):
                    if third != column and third != other:
                        term = term * (node_points - node_points[third]) / (node_points[column] - node_points[third])
                derivative[:, column] += term
    stiffness = derivative.T @ (weights[:, None] * derivative)
    stiffness[0, 0] += TAU
    stiffness[3, 3] += TAU
    scale = weights ** (-0.5)
    eigen_values, eigen_vectors = jacobi_eigen(scale[:, None] * stiffness * scale[None, :])
    modes = scale[:, None] * eigen_vectors
    prolongation = np.stack([lagrange((node_points - 1.0) / 2.0, node_points), lagrange((node_points + 1.0) / 2.0, node_points)])
    return (jnp.asarray(stiffness, jnp.float32), jnp.asarray(weights, jnp.float32), jnp.asarray(eigen_values, jnp.float32), jnp.asarray(modes, jnp.float32), jnp.asarray(prolongation, jnp.float32))

def level_scales(level_index):
    size_x = 2.0 ** level_index
    size_y = 2.0 ** min(level_index, LOC)
    return (size_y * size_y / size_x, size_x * size_y / size_y, size_x * size_y / size_y, size_x * size_y * size_y)

def coarse_axes(level_index):
    if level_index < LOC:
        return (0, 1, 2)
    return (0,)

def along(matrix, vector, axis):
    if axis == 0:
        return jnp.einsum('ai,ijkxyz->ajkxyz', matrix, vector, precision=EXACT)
    if axis == 1:
        return jnp.einsum('aj,ijkxyz->iakxyz', matrix, vector, precision=EXACT)
    return jnp.einsum('ak,ijkxyz->ijaxyz', matrix, vector, precision=EXACT)

def invert(source, coefficient, level_index):
    stiffness, weights, eigen_values, modes, prolongation = tables()
    wide_x, wide_y, wide_z, volume = level_scales(level_index)
    spectrum = wide_x * eigen_values[:, None, None] + wide_y * eigen_values[None, :, None] + wide_z * eigen_values[None, None, :]
    projected = along(modes.T, along(modes.T, along(modes.T, source, 0), 1), 2)
    scaled = projected / (coefficient * spectrum[:, :, :, None, None, None] + SHIFT * volume)
    return along(modes, along(modes, along(modes, scaled, 0), 1), 2)

def orient(trace, code):
    turned = jnp.where(code % 2 == 1, jnp.swapaxes(trace, 0, 1), trace)
    turned = jnp.where(code // 2 % 2 == 1, jnp.flip(turned, 0), turned)
    return jnp.where(code // 4 == 1, jnp.flip(turned, 1), turned)

def operate(vector, coefficient, level_index, neighbours):
    stiffness, weights, eigen_values, modes, prolongation = tables()
    wide_x, wide_y, wide_z, volume = level_scales(level_index)
    face_mass = weights[:, None] * weights[None, :]
    cell_mass = face_mass[:, :, None] * weights[None, None, :]
    inner = wide_x * face_mass[None, :, :, None, None, None] * along(stiffness, vector, 0)
    inner = inner + wide_y * face_mass[:, None, :, None, None, None] * along(stiffness, vector, 1)
    inner = inner + wide_z * face_mass[:, :, None, None, None, None] * along(stiffness, vector, 2)
    sheet = -TAU * face_mass[:, :, None, None, None]
    inner = inner.at[0].add(wide_x * sheet * neighbours[0])
    inner = inner.at[3].add(wide_x * sheet * neighbours[1])
    inner = inner.at[:, 0].add(wide_y * sheet * neighbours[2])
    inner = inner.at[:, 3].add(wide_y * sheet * neighbours[3])
    inner = inner.at[:, :, 0].add(wide_z * sheet * neighbours[4])
    inner = inner.at[:, :, 3].add(wide_z * sheet * neighbours[5])
    return coefficient * inner + SHIFT * volume * cell_mass[:, :, :, None, None, None] * vector

def rolled(vector):
    return (jnp.roll(vector[3], 1, axis=2), jnp.roll(vector[0], -1, axis=2), jnp.roll(vector[:, 3], 1, axis=3), jnp.roll(vector[:, 0], -1, axis=3), jnp.roll(vector[:, :, 3], 1, axis=4), jnp.roll(vector[:, :, 0], -1, axis=4))

def restrict(vector, level_index):
    prolongation = tables()[4]
    forms = ('cab,ajkxcyz->bjkxyz', 'cab,iakxycz->ibkxyz', 'cab,ijaxyzc->ijbxyz')
    for axis in coarse_axes(level_index):
        shape = vector.shape
        split = shape[:3 + axis] + (shape[3 + axis] // 2, 2) + shape[4 + axis:]
        vector = jnp.einsum(forms[axis], prolongation, vector.reshape(split), precision=EXACT)
    return vector

def extend(vector, level_index):
    prolongation = tables()[4]
    forms = ('cab,bjkxyz->ajkxcyz', 'cab,ibkxyz->iakxycz', 'cab,ijbxyz->ijaxyzc')
    for axis in coarse_axes(level_index):
        shape = vector.shape
        merged = shape[:3 + axis] + (shape[3 + axis] * 2,) + shape[4 + axis:]
        vector = jnp.einsum(forms[axis], prolongation, vector, precision=EXACT).reshape(merged)
    return vector

def coarsen_coefficient(coefficient, level_index):
    for axis in coarse_axes(level_index):
        shape = coefficient.shape
        split = coefficient.reshape(shape[:axis] + (shape[axis] // 2, 2) + shape[axis + 1:])
        first = lax.index_in_dim(split, 0, axis + 1, keepdims=False)
        second = lax.index_in_dim(split, 1, axis + 1, keepdims=False)
        coefficient = (first + second) * 0.5
    return coefficient

def cycle(level_index, source, coefficient, orientation):

    def apply_operator(vector):
        traces = rolled(vector)
        if level_index == 0:
            traces = tuple((orient(traces[face], orientation[face]) for face in range(6)))
        return operate(vector, coefficient, level_index, traces)
    result = OMEGA * invert(source, coefficient, level_index)
    result = result + OMEGA * invert(source - apply_operator(result), coefficient, level_index)
    if level_index < LOC + AGG:
        coarse = restrict(source - apply_operator(result), level_index)
        correction = cycle(level_index + 1, coarse, coarsen_coefficient(coefficient, level_index), orientation)
        result = result + extend(correction, level_index)
        for sweep_index in range(2):
            result = result + OMEGA * invert(source - apply_operator(result), coefficient, level_index)
    return result

def reference(source, coefficient, orientation):
    return cycle(0, source, coefficient, orientation)
```

```python
import math

import jax
import jax.numpy as jnp
import numpy as np
from jax import lax
from jax.experimental import pallas as pl
from jax.experimental.pallas import tpu as pltpu
from jax.sharding import PartitionSpec as P

LOC = 2
TAU = 6.0
SHIFT = 1.0
OMEGA = 0.8
KEEP = 0.2
MESH = pl.DeviceIdType.MESH
F32 = jnp.float32


def lagrange(points, node_points):
    table = np.ones((points.shape[0], 4))
    for column in range(4):
        for other in range(4):
            if other != column:
                table[:, column] *= (points - node_points[other]) / (
                    node_points[column] - node_points[other]
                )
    return table


def jacobi_eigen(matrix):
    current = matrix.copy()
    vectors = np.eye(4)
    for sweep in range(12):
        for first in range(3):
            for second in range(first + 1, 4):
                angle = 0.5 * math.atan2(
                    2.0 * current[first, second], current[second, second] - current[first, first]
                )
                cosine = math.cos(angle)
                sine = math.sin(angle)
                rotation = np.eye(4)
                rotation[first, first] = cosine
                rotation[second, second] = cosine
                rotation[first, second] = sine
                rotation[second, first] = -sine
                current = rotation.T @ current @ rotation
                vectors = vectors @ rotation
    return (np.array([current[index, index] for index in range(4)]), vectors)


def tables():
    node_points = np.array([-1.0, -1.0 / math.sqrt(5.0), 1.0 / math.sqrt(5.0), 1.0])
    weights = np.array([1.0, 5.0, 5.0, 1.0]) / 6.0
    derivative = np.zeros((4, 4))
    for column in range(4):
        for other in range(4):
            if other != column:
                term = np.full(4, 1.0 / (node_points[column] - node_points[other]))
                for third in range(4):
                    if third != column and third != other:
                        term = (
                            term
                            * (node_points - node_points[third])
                            / (node_points[column] - node_points[third])
                        )
                derivative[:, column] += term
    stiffness = derivative.T @ (weights[:, None] * derivative)
    stiffness[0, 0] += TAU
    stiffness[3, 3] += TAU
    scale = weights ** (-0.5)
    eigen_values, eigen_vectors = jacobi_eigen(scale[:, None] * stiffness * scale[None, :])
    modes = scale[:, None] * eigen_vectors
    order = sorted(range(4), key=lambda mode: eigen_values[mode])
    eigen_values, modes = (eigen_values[order], modes[:, order])
    child = lagrange((node_points - 1.0) / 2.0, node_points)
    transfer = modes.T @ (weights[:, None] * (child @ modes))
    return (eigen_values, modes, transfer)


LAM, MODES, TRANSFER = tables()
PAR = (1.0, -1.0, 1.0, -1.0)
SIG = MODES[0]
SQ = [float(value * value) for value in SIG]
INTO = SIG[:, None] * MODES.T
MID = [float(MODES[1, mode] / SIG[mode]) for mode in range(4)]
REST = SIG[:, None] * TRANSFER.T / SIG[None, :]
EXT = SIG[:, None] * TRANSFER / SIG[None, :]


def level_scales(level):
    size_x = 2.0**level
    size_y = 2.0 ** min(level, LOC)
    return (size_y * size_y / size_x, size_x, size_x, size_x * size_y * size_y)


def roll(value, shift, axis):
    size = value.shape[axis]
    shift = shift % size
    if shift == 0:
        return value
    return pltpu.roll(value, shift, axis % value.ndim)


def iota(shape, axis):
    return lax.broadcasted_iota(jnp.int32, shape, axis)


def combine(row, parts):
    total = None
    for factor, part in zip(row, parts):
        term = part * float(factor)
        total = term if total is None else total + term
    return total


def into_modes(s0, s1, s2, s3):
    e0, e1, o0, o1 = (s0 + s3, s1 + s2, s0 - s3, s1 - s2)
    return [
        combine((INTO[mode, 0], INTO[mode, 1]), (e0, e1) if PAR[mode] > 0 else (o0, o1))
        for mode in range(4)
    ]


def from_modes(x0, x1, x2, x3):
    even, odd = (x0 + x2, x1 + x3)
    inner_even = x0 * MID[0] + x2 * MID[2]
    inner_odd = x1 * MID[1] + x3 * MID[3]
    return [even + odd, inner_even + inner_odd, inner_even - inner_odd, even - odd]


def restrict4(first, second):
    plus = [a + b for a, b in zip(first, second)]
    minus = [a - b for a, b in zip(first, second)]
    even = (plus[0], minus[1], plus[2], minus[3])
    odd = (minus[0], plus[1], minus[2], plus[3])
    return [combine(REST[mode], even if PAR[mode] > 0 else odd) for mode in range(4)]


def extend4(parts, sign):
    x0, x1, x2, x3 = parts
    out = []
    for mode in range(4):
        same, other = ((x0, x2), (x1, x3))
        row_same, row_other = ((EXT[mode, 0], EXT[mode, 2]), (EXT[mode, 1], EXT[mode, 3]))
        if PAR[mode] < 0:
            same, other, row_same, row_other = (other, same, row_other, row_same)
        out.append(combine(row_same, same) + sign * combine(row_other, other))
    return out


def extend4_pair(parts):
    x0, x1, x2, x3 = parts
    low, high = ([], [])
    for mode in range(4):
        same, other = ((x0, x2), (x1, x3))
        row_same, row_other = ((EXT[mode, 0], EXT[mode, 2]), (EXT[mode, 1], EXT[mode, 3]))
        if PAR[mode] < 0:
            same, other, row_same, row_other = (other, same, row_other, row_same)
        a, b = (combine(row_same, same), combine(row_other, other))
        low.append(a + b)
        high.append(a - b)
    return low, high


def inverse_tables(g_ref, d_ref, coefficient, level):
    wide_x, wide_y, wide_z, volume = level_scales(level)
    done = {}
    for i in range(4):
        for j in range(4):
            for k in range(4):
                key = (i,) + tuple(sorted((j, k)))
                if wide_x == wide_y:
                    key = tuple(sorted((i, j, k)))
                if key not in done:
                    spectrum = float(wide_x * LAM[i] + wide_y * LAM[j] + wide_z * LAM[k])
                    diagonal = coefficient * spectrum + SHIFT * volume
                    done[key] = (OMEGA / diagonal, diagonal)
                g_ref[i, j, k] = done[key][0]
                d_ref[i, j, k] = done[key][1]


def first_guess(x_ref, b_ref, g_ref):
    for i in range(4):
        for j in range(4):
            x_ref[i, j] = g_ref[i, j] * b_ref[i, j]


def face_pair(x_ref, axis, line):
    if axis == 0:
        parts = [x_ref[mode, line] for mode in range(4)]
    elif axis == 1:
        parts = [x_ref[line, mode] for mode in range(4)]
    else:
        parts = [x_ref[line, :, mode] for mode in range(4)]
    even, odd = (parts[0] + parts[2], parts[1] + parts[3])
    return even + odd, even - odd


def flux(b_ref, f_ref, i, j):
    add = b_ref[i, j] + f_ref[0, i % 2, j] * SQ[i] + f_ref[1, j % 2, i] * SQ[j]
    along_z = [f_ref[2, k % 2, i, j] * SQ[k] for k in range(4)]
    return add + jnp.stack(along_z, axis=0)


def sweep(x_ref, b_ref, g_ref, f_ref):
    for i in range(4):
        for j in range(4):
            x_ref[i, j] = x_ref[i, j] * KEEP + g_ref[i, j] * flux(b_ref, f_ref, i, j)


def residual(r_ref, x_ref, b_ref, d_ref, f_ref):
    for i in range(4):
        for j in range(4):
            r_ref[i, j] = flux(b_ref, f_ref, i, j) - d_ref[i, j] * x_ref[i, j]


class Halo:
    def __init__(self, rows, stride, x, b, g, d, r, t, f, coefficient, wide, orientation, signs):
        self.rows, self.stride = (rows, stride)
        self.x, self.b, self.g, self.d, self.r, self.t, self.f = (x, b, g, d, r, t, f)
        self.coefficient, self.wide = (coefficient, wide)
        self.orientation, self.signs = (orientation, signs)

    def send(self, link):
        rows, stride = (self.rows, self.stride)
        low_rows = iota((4, 8, 128), 1) < 4
        lane = iota((rows, 128), 1)
        firsts, lasts = ([], [])
        for j in range(4):
            low, high = face_pair(self.x, 0, j)
            up, down = (roll(high, 4, 1), roll(low, rows - 4, 1))
            self.t[0, 0, j] = up
            self.t[0, 1, j] = down
            firsts.append((up[:, :8], low[:, :8]))
            lasts.append((high[:, rows - 8 :], down[:, rows - 8 :]))
        for j in range(2):
            link.px[0, j] = jnp.where(low_rows, firsts[j][0], lasts[j + 2][0])
            link.px[1, j] = jnp.where(low_rows, firsts[j][1], lasts[j + 2][1])
        link.start_x()
        packed_high = packed_low = jnp.zeros((rows, 128), F32)
        for i in range(4):
            low, high = face_pair(self.x, 2, i)
            self.t[2, 0, i] = roll(high, stride, 2)
            self.t[2, 1, i] = roll(low, 128 - stride, 2)
            for j in range(4):
                spot = 4 * i + j
                packed_high = jnp.where(lane == spot, roll(high[j], spot + stride, 1), packed_high)
                packed_low = jnp.where(lane == spot, roll(low[j], spot, 1), packed_low)
        link.pz[0] = packed_high
        link.pz[1] = packed_low
        link.start_z()
        for i in range(4):
            low, high = face_pair(self.x, 1, i)
            self.t[1, 0, i] = roll(high, stride, 1)
            self.t[1, 1, i] = roll(low, rows - stride, 1)
            link.py[0, i] = high
            link.py[1, i] = low
        link.start_y()

    def merge(self, axis):
        rows = self.rows
        factor = (TAU * self.wide * self.coefficient[...])[None]
        for line in range(4):
            pair = []
            for side in range(2):
                value = self.t[axis, side, line]
                if self.orientation is not None:
                    face = 2 * axis + side
                    swap = jnp.broadcast_to(self.orientation[face][None], (4, rows, 128)) % 2 == 1
                    value = jnp.where(swap, self.t[axis, side, :, line], value)
                    value = value * self.signs[face, line % 2]
                pair.append(value)
            self.f[axis, 0, line] = factor * (pair[0] + pair[1])
            self.f[axis, 1, line] = factor * (pair[0] - pair[1])

    def receive(self, link):
        rows, stride = (self.rows, self.stride)
        link.wait_y()
        inner = iota((4, rows, 128), 1) % 4
        back = 4 - stride
        for i in range(4):
            self.t[1, 0, i] = jnp.where(inner == 0, roll(link.qy[0, i], rows - back, 1), self.t[1, 0, i])
            self.t[1, 1, i] = jnp.where(inner == back, roll(link.qy[1, i], back, 1), self.t[1, 1, i])
        self.merge(1)
        link.wait_z()
        lane = iota((rows, 128), 1)
        high, low = (link.qz[0], link.qz[1])
        for i in range(4):
            for j in range(4):
                spot = 4 * i + j
                self.t[2, 0, i, j] = jnp.where(lane == 0, roll(high, 128 - spot, 1), self.t[2, 0, i, j])
                self.t[2, 1, i, j] = jnp.where(
                    lane == 128 - stride, roll(low, 128 - stride - spot, 1), self.t[2, 1, i, j]
                )
        self.merge(2)
        link.wait_x()
        low_rows = iota((4, 8, 128), 1) < 4
        for j in range(4):
            high, low = (link.qx[0, j % 2], link.qx[1, j % 2])
            if j < 2:
                low = roll(low, 4, 1)
            else:
                high = roll(high, 4, 1)
            self.t[0, 0, j, :, :8] = jnp.where(low_rows, high, self.t[0, 0, j, :, :8])
            self.t[0, 1, j, :, rows - 8 :] = jnp.where(low_rows, self.t[0, 1, j, :, rows - 8 :], low)
        self.merge(0)

    def smooth(self, link):
        self.send(link)
        self.receive(link)
        sweep(self.x, self.b, self.g, self.f)

    def defect(self, link):
        self.send(link)
        self.receive(link)
        residual(self.r, self.x, self.b, self.d, self.f)


class Link:
    def __init__(self, px, qx, py, qy, pz, qz, send, recv, at):
        self.px, self.qx, self.py, self.qy, self.pz, self.qz = (px, qx, py, qy, pz, qz)
        gx, gy, gz = at

        def copy(src, dst, spot, device):
            return pltpu.make_async_remote_copy(
                src_ref=src,
                dst_ref=dst,
                send_sem=send.at[spot],
                recv_sem=recv.at[spot],
                device_id=device,
                device_id_type=MESH,
            )

        self.x_copies = [
            copy(px.at[0], qx.at[0], 0, {"gx": lax.rem(gx + 1, 32)}),
            copy(px.at[1], qx.at[1], 1, {"gx": lax.rem(gx + 31, 32)}),
        ]
        self.z_copies = [
            copy(pz.at[0], qz.at[0], 2, {"gz": lax.rem(gz + 1, 4)}),
            copy(pz.at[1], qz.at[1], 3, {"gz": lax.rem(gz + 3, 4)}),
        ]
        self.y_copies = [copy(py, qy, 4, {"gy": 1 - gy})]

    def start_x(self):
        for item in self.x_copies:
            item.start()

    def start_y(self):
        for item in self.y_copies:
            item.start()

    def start_z(self):
        for item in self.z_copies:
            item.start()

    def wait_x(self):
        for item in self.x_copies:
            item.wait_recv()

    def wait_y(self):
        for item in self.y_copies:
            item.wait_recv()

    def wait_z(self):
        for item in self.z_copies:
            item.wait_recv()

    def close(self):
        for item in self.x_copies + self.y_copies + self.z_copies:
            item.wait_send()


class Whole:
    def __init__(self, level, count, x, b, g, d, r, f, coefficient):
        self.level, self.count = (level, count)
        self.x, self.b, self.g, self.d, self.r, self.f = (x, b, g, d, r, f)
        self.coefficient = coefficient

    def faces(self):
        wide_x, wide_y, wide_z, _ = level_scales(self.level)
        count = self.count
        coefficient = self.coefficient[...][None]
        ends = iota((4, count, 8, 128), 3) % 64
        for line in range(4):
            low, high = face_pair(self.x, 0, line)
            before, after = (roll(high[:, count - 1 :], 1, 2), roll(low[:, :1], 7, 2))
            if count > 1:
                before = jnp.concatenate([before, high[:, : count - 1]], axis=1)
                after = jnp.concatenate([low[:, 1:], after], axis=1)
            factor = coefficient * (TAU * wide_x)
            self.f[0, 0, line] = factor * (before + after)
            self.f[0, 1, line] = factor * (before - after)
            low, high = face_pair(self.x, 1, line)
            factor = coefficient * (TAU * wide_y)
            self.f[1, 0, line] = factor * roll(high + low, 64, 3)
            self.f[1, 1, line] = factor * roll(high - low, 64, 3)
            low, high = face_pair(self.x, 2, line)
            factor = coefficient * (TAU * wide_z)
            before = jnp.where(ends < 4, roll(high, 69, 3), roll(high, 4, 3))
            after = jnp.where(ends >= 60, roll(low, 59, 3), roll(low, 124, 3))
            self.f[2, 0, line] = factor * (before + after)
            self.f[2, 1, line] = factor * (before - after)

    def tables(self):
        inverse_tables(self.g, self.d, self.coefficient[...], self.level)

    def before(self):
        first_guess(self.x, self.b, self.g)
        self.faces()
        sweep(self.x, self.b, self.g, self.f)

    def down(self, coarse):
        self.faces()
        residual(self.r, self.x, self.b, self.d, self.f)
        for j in range(4):
            for block in range(coarse.count):
                first = [self.r[i, j, :, 2 * block] for i in range(4)]
                second = [self.r[i, j, :, 2 * block + 1] for i in range(4)]
                for i, value in enumerate(restrict4(first, second)):
                    coarse.b[i, j, :, block] = value

    def up(self, coarse):
        for j in range(4):
            for block in range(coarse.count):
                low, high = extend4_pair([coarse.x[i, j, :, block] for i in range(4)])
                for i in range(4):
                    self.x[i, j, :, 2 * block] += low[i]
                    self.x[i, j, :, 2 * block + 1] += high[i]
        for step in range(2):
            self.faces()
            sweep(self.x, self.b, self.g, self.f)


def kernel(
    source,
    coefficient,
    orientation,
    out,
    x0, b0, g0, d0, r0, t0, f0, signs,
    x1, b1, g1, d1, r1, t1, f1, c1, w1, v1,
    x2, b2, g2, d2, r2, f2, c2,
    x3, b3, g3, d3, r3, f3, c3,
    x4, b4, g4, d4, r4, f4, c4,
    px, qx, py0, qy0, pz0, qz0, py1, qy1, pz1, qz1,
    cs, call, cown, cin,
    ms, mall, my, mz,
    face_send, face_recv,
    c_send, c_recv, c_send2, c_recv2,
    m_send, m_recv, m_send2, m_recv2,
):
    gx, gy, gz = (lax.axis_index("gx"), lax.axis_index("gy"), lax.axis_index("gz"))
    slow, fast = (gx // 4, lax.rem(gx, 4))
    slow_at = pl.multiple_of(slow * 16, 16)
    slow_at8 = pl.multiple_of(slow * 8, 8)
    offsets = [(a, b) for a in range(8) for b in range(4) if (a, b) != (0, 0)]

    def along_x(a, b):
        return {"gx": lax.rem(slow + a, 8) * 4 + lax.rem(fast + b, 4)}

    up_z, down_z = (lax.rem(gz + 1, 4), lax.rem(gz + 3, 4))
    around = [
        {"gy": 1 - gy},
        {"gz": up_z},
        {"gy": 1 - gy, "gz": up_z},
        {"gz": down_z},
        {"gy": 1 - gy, "gz": down_z},
    ]

    barrier = pltpu.get_barrier_semaphore()
    for a, b in offsets:
        pl.semaphore_signal(barrier, inc=1, device_id=along_x(a, b), device_id_type=MESH)
    for device in around:
        pl.semaphore_signal(barrier, inc=1, device_id=device, device_id_type=MESH)

    for i in range(4):
        for k, value in enumerate(into_modes(*[source[i, :, k] for k in range(4)])):
            b0[i, :, k] = value
    for i in range(4):
        for j, value in enumerate(into_modes(*[b0[i, j] for j in range(4)])):
            b0[i, j] = value
    for j in range(4):
        for i, value in enumerate(into_modes(*[b0[i, j] for i in range(4)])):
            b0[i, j] = value
    inverse_tables(g0, d0, coefficient[...], 0)
    first_guess(x0, b0, g0)
    for face in range(6):
        code = orientation[face]
        one = jnp.ones((16, 128), F32)
        first = jnp.where(code // 2 % 2 == 1, -one, one)
        second = jnp.where(code // 4 == 1, -one, one)
        signs[face, 0] = jnp.stack([one, second, one, second], axis=0)
        signs[face, 1] = jnp.stack([first, first * second, first, first * second], axis=0)

    row8 = iota((8, 128), 0)
    lane8 = iota((8, 128), 1)
    top, bottom = (coefficient[:8], coefficient[8:])
    value = 0.5 * (
        jnp.where(row8 < 4, top, roll(bottom, 4, 0)) + jnp.where(row8 < 4, roll(top, 4, 0), bottom)
    )
    value = 0.5 * (value + roll(value, 7, 0))
    value = 0.5 * (value + roll(value, 127, 1))
    c1[...] = value
    inverse_tables(g1, d1, value, 1)
    value = 0.5 * (value + roll(value, 4, 0))
    value = 0.5 * (value + roll(value, 6, 0))
    cs[...] = 0.5 * (value + roll(value, 126, 1))

    pl.semaphore_wait(barrier, 36)

    def link(level, step):
        spot = 4 * level + step
        py, qy, pz, qz = (py0, qy0, pz0, qz0) if level == 0 else (py1, qy1, pz1, qz1)
        return Link(
            px.at[spot], qx.at[spot], py.at[step], qy.at[step], pz.at[step], qz.at[step],
            face_send.at[spot], face_recv.at[spot], (gx, gy, gz),
        )

    def copy(src, dst, send, recv, device):
        return pltpu.make_async_remote_copy(
            src_ref=src, dst_ref=dst, send_sem=send, recv_sem=recv, device_id=device, device_id_type=MESH
        )

    fine = Halo(16, 1, x0, b0, g0, d0, r0, t0, f0, coefficient, 1.0, orientation, signs)
    mid = Halo(8, 2, x1, b1, g1, d1, r1, t1, f1, c1, 2.0, None, None)
    links = []

    links.append(link(0, 0))
    fine.send(links[-1])
    c_copies = [
        copy(cs, call.at[fast, pl.ds(slow_at8, 8)], c_send.at[a, b], c_recv.at[a, b], along_x(a, b))
        for a, b in offsets
    ]
    for item in c_copies:
        item.start()
    call[fast, pl.ds(slow_at8, 8), :] = cs[...]
    fine.receive(links[-1])
    sweep(x0, b0, g0, f0)
    links.append(link(0, 1))
    fine.send(links[-1])
    for item in c_copies:
        item.wait_recv()
    for block in range(4):
        cown[block] = call[block, pl.ds(0, 8, stride=8), :]
    c_around = [
        copy(cown, cin.at[spot], c_send2.at[spot], c_recv2.at[spot], device)
        for spot, device in enumerate(around)
    ]
    for item in c_around:
        item.start()
    fine.receive(links[-1])
    residual(r0, x0, b0, d0, f0)
    row4 = iota((4, 8, 128), 1)
    lane4 = iota((4, 8, 128), 2)
    for j in range(4):
        first, second = ([], [])
        for i in range(4):
            top, bottom = (r0[i, j, :, :8], r0[i, j, :, 8:])
            first.append(jnp.where(row4 < 4, top, roll(bottom, 4, 1)))
            second.append(jnp.where(row4 < 4, roll(top, 4, 1), bottom))
        for i, value in enumerate(restrict4(first, second)):
            w1[i, j] = value
    for i in range(4):
        first = [w1[i, j] for j in range(4)]
        for j, value in enumerate(restrict4(first, [roll(item, 7, 1) for item in first])):
            v1[i, j] = value
    for i in range(4):
        first = [v1[i, :, k] for k in range(4)]
        for k, value in enumerate(restrict4(first, [roll(item, 127, 2) for item in first])):
            b1[i, :, k] = value

    first_guess(x1, b1, g1)
    links.append(link(1, 0))
    mid.send(links[-1])
    for item in c_around:
        item.wait_recv()
    for block in range(4):
        mine, other = (cown[block], cin[0, block])
        below, below_other, above, above_other = (cin[spot, block] for spot in range(1, 5))
        phase = lane8 % 4
        near = jnp.where(phase == 0, roll(below, 64, 1), roll(mine, 1, 1))
        near = jnp.where(phase == 2, roll(mine, 66, 1), near)
        near = jnp.where(phase == 3, roll(above, 3, 1), near)
        far = jnp.where(phase == 0, below_other, roll(other, 65, 1))
        far = jnp.where(phase == 2, roll(other, 2, 1), far)
        far = jnp.where(phase == 3, roll(above_other, 67, 1), far)
        c2[block] = jnp.where(lane8 < 64, near, far)
    for block in range(2):
        c3[block] = 0.5 * (c2[2 * block] + c2[2 * block + 1])
    c4[0] = 0.5 * (c3[0] + c3[1])
    level2 = Whole(2, 4, x2, b2, g2, d2, r2, f2, c2)
    level3 = Whole(3, 2, x3, b3, g3, d3, r3, f3, c3)
    level4 = Whole(4, 1, x4, b4, g4, d4, r4, f4, c4)
    level2.tables()
    mid.receive(links[-1])
    sweep(x1, b1, g1, f1)
    links.append(link(1, 1))
    mid.send(links[-1])
    level3.tables()
    level4.tables()
    mid.receive(links[-1])
    residual(r1, x1, b1, d1, f1)
    for j in range(4):
        first = [r1[i, j] for i in range(4)]
        for i, value in enumerate(restrict4(first, [roll(item, 4, 1) for item in first])):
            w1[i, j] = value
    for i in range(4):
        first = [w1[i, j] for j in range(4)]
        for j, value in enumerate(restrict4(first, [roll(item, 6, 1) for item in first])):
            v1[i, j] = value
    packed = []
    for i in range(4):
        first = [v1[i, :, k] for k in range(4)]
        total = None
        for k, value in enumerate(restrict4(first, [roll(item, 126, 2) for item in first])):
            total = value if k == 0 else jnp.where(lane4 % 4 == k, roll(value, k, 2), total)
        packed += [total[j] for j in range(4)]
    for line in range(8):
        low, high = (packed[line], packed[line + 8])
        ms[pl.ds(line, 1), :] = jnp.where(lane8 < 64, low, roll(high, 64, 1))[:1]
        ms[pl.ds(line + 8, 1), :] = jnp.where(lane8 < 64, roll(low, 64, 1), high)[:1]

    m_copies = {
        (a, b): copy(ms, mall.at[fast, pl.ds(slow_at, 16)], m_send.at[a, b], m_recv.at[a, b], along_x(a, b))
        for a, b in offsets
    }
    for item in m_copies.values():
        item.start()
    mall[fast, pl.ds(slow_at, 16), :] = ms[...]
    passed = []
    for a in range(8):
        for b in range(4):
            if (a, b) != (0, 0):
                m_copies[a, b].wait_recv()
        start = lax.rem(slow + 8 - a, 8)
        start16 = pl.multiple_of(start * 16, 16)
        start8 = pl.multiple_of(start * 8, 8)
        upper = pl.multiple_of(start * 16 + 8, 8)
        for spot, device in enumerate(around):
            if spot == 0:
                src, dst = (mall.at[:, pl.ds(start16, 16)], my.at[:, pl.ds(start16, 16)])
            else:
                src = mall.at[:, pl.ds(upper if spot < 3 else start16, 8)]
                dst = mz.at[spot - 1, :, pl.ds(start8, 8)]
            item = copy(src, dst, m_send2.at[spot, a], m_recv2.at[spot, a], device)
            item.start()
            passed.append(item)
    for item in passed:
        item.wait_recv()

    def unpack(block, carry):
        odd, pair = (lane8 % 2 == 1, lane8 % 4 >= 2)
        for line in range(8):
            def rows(ref, start, stride):
                return ref[block, pl.ds(start, 8, stride=stride), :]

            near = [
                rows(mz.at[0], line, 8), rows(mall, line, 16), rows(mall, line + 8, 16), rows(mz.at[2], line, 8)
            ]
            far = [
                rows(mz.at[1], line, 8), rows(my, line, 16), rows(my, line + 8, 16), rows(mz.at[3], line, 8)
            ]
            for half in range(2):
                if half == 0:
                    part = [jnp.where(lane8 < 64, a, roll(b, 64, 1)) for a, b in zip(near, far)]
                else:
                    part = [jnp.where(lane8 < 64, roll(a, 64, 1), b) for a, b in zip(near, far)]
                step = [
                    jnp.where(odd, roll(part[1], 1, 1), part[0]),
                    jnp.where(odd, part[1], roll(part[0], 127, 1)),
                    jnp.where(odd, roll(part[3], 1, 1), part[2]),
                    jnp.where(odd, part[3], roll(part[2], 127, 1)),
                ]
                last = [
                    jnp.where(pair, roll(step[2], 2, 1), step[0]),
                    jnp.where(pair, roll(step[3], 2, 1), step[1]),
                    jnp.where(pair, step[2], roll(step[0], 126, 1)),
                    jnp.where(pair, step[3], roll(step[1], 126, 1)),
                ]
                mode = line + 8 * half
                for k in range(4):
                    b2[mode // 4, mode % 4, k, block] = last[k]
        return carry

    lax.fori_loop(0, 4, unpack, 0)
    level2.before()
    level2.down(level3)
    level3.before()
    level3.down(level4)
    level4.before()
    level3.up(level4)
    level2.up(level3)

    for i in range(4):
        for j in range(4):
            own = jnp.broadcast_to(x2[i, j, :, fast, pl.ds(slow, 1), :], (4, 8, 128))
            own = jnp.where(lane4 < 64, roll(own, 127, 2), roll(own, 62, 2))
            w1[i, j] = jnp.where(lane4 % 4 < 2, own, roll(own, 2, 2))
    one = jnp.ones((4, 8, 128), F32)
    sign = jnp.where(lane4 % 4 < 2, one, -one)
    for i in range(4):
        for k, value in enumerate(extend4([w1[i, :, k] for k in range(4)], sign)):
            w1[i, :, k] = value
    sign = jnp.where(row4 % 4 < 2, one, -one)
    for i in range(4):
        for j, value in enumerate(extend4([w1[i, j] for j in range(4)], sign)):
            w1[i, j] = value
    sign = jnp.where(row4 < 4, one, -one)
    for j in range(4):
        for i, value in enumerate(extend4([w1[i, j] for i in range(4)], sign)):
            x1[i, j] += value
    for step in range(2):
        links.append(link(1, 2 + step))
        mid.smooth(links[-1])

    for i in range(4):
        for j in range(4):
            own = x1[i, j]
            own = jnp.where(row4 % 2 == 0, own, roll(own, 1, 1))
            w1[i, j] = jnp.where(lane4 % 2 == 0, own, roll(own, 1, 2))
    sign = jnp.where(lane4 % 2 == 0, one, -one)
    for i in range(4):
        for k, value in enumerate(extend4([w1[i, :, k] for k in range(4)], sign)):
            w1[i, :, k] = value
    sign = jnp.where(row4 % 2 == 0, one, -one)
    for i in range(4):
        for j, value in enumerate(extend4([w1[i, j] for j in range(4)], sign)):
            w1[i, j] = value
    for j in range(4):
        parts = []
        for i in range(4):
            own = w1[i, j]
            turned = roll(own, 4, 1)
            low, high = (jnp.where(row4 < 4, own, turned), jnp.where(row4 < 4, turned, own))
            parts.append(jnp.concatenate([low, high], axis=1))
        wide_one = jnp.ones((4, 16, 128), F32)
        sign = jnp.where(iota((4, 16, 128), 1) % 8 < 4, wide_one, -wide_one)
        for i, value in enumerate(extend4(parts, sign)):
            x0[i, j] += value
    for step in range(2):
        links.append(link(0, 2 + step))
        fine.smooth(links[-1])

    for i in range(4):
        for k, value in enumerate(from_modes(*[x0[i, :, k] for k in range(4)])):
            out[i, :, k] = value
    for i in range(4):
        for j, value in enumerate(from_modes(*[out[i, j] for j in range(4)])):
            out[i, j] = value
    for j in range(4):
        for i, value in enumerate(from_modes(*[out[i, j] for i in range(4)])):
            out[i, j] = value

    for item in links:
        item.close()
    for item in c_copies + c_around + list(m_copies.values()) + passed:
        item.wait_send()


def scratch():
    def mem(*shape):
        return pltpu.VMEM(shape, F32)

    modes = (4, 4, 4)
    level0 = [mem(*modes, 16, 128)] * 5 + [
        mem(3, 2, 4, 4, 16, 128), mem(3, 2, 4, 4, 16, 128), mem(6, 2, 4, 16, 128)
    ]
    level1 = [mem(*modes, 8, 128)] * 5 + [
        mem(3, 2, 4, 4, 8, 128), mem(3, 2, 4, 4, 8, 128), mem(8, 128), mem(*modes, 8, 128), mem(*modes, 8, 128)
    ]
    whole = []
    for count in (4, 2, 1):
        whole += [mem(*modes, count, 8, 128)] * 5 + [mem(3, 2, 4, 4, count, 8, 128), mem(count, 8, 128)]
    faces = [
        mem(8, 2, 2, 4, 8, 128), mem(8, 2, 2, 4, 8, 128),
        mem(4, 2, 4, 4, 16, 128), mem(4, 2, 4, 4, 16, 128), mem(4, 2, 16, 128), mem(4, 2, 16, 128),
        mem(4, 2, 4, 4, 8, 128), mem(4, 2, 4, 4, 8, 128), mem(4, 2, 8, 128), mem(4, 2, 8, 128),
    ]
    gathered = [
        mem(8, 128), mem(4, 64, 128), mem(4, 8, 128), mem(5, 4, 8, 128),
        mem(16, 128), mem(4, 128, 128), mem(4, 128, 128), mem(4, 4, 64, 128),
    ]
    dma = pltpu.SemaphoreType.DMA
    sems = [dma((8, 5)), dma((8, 5)), dma((8, 4)), dma((8, 4)), dma((5,)), dma((5,)),
            dma((8, 4)), dma((8, 4)), dma((5, 8)), dma((5, 8))]
    return level0 + level1 + whole + faces + gathered + sems


def local(source, coefficient, orientation):
    vmem = pl.BlockSpec(memory_space=pltpu.VMEM)
    out = pl.pallas_call(
        kernel,
        out_shape=jax.ShapeDtypeStruct((4, 4, 4, 16, 128), F32),
        in_specs=[vmem] * 3,
        out_specs=vmem,
        scratch_shapes=scratch(),
        compiler_params=pltpu.CompilerParams(
            collective_id=0, has_side_effects=True, vmem_limit_bytes=44 * 1024 * 1024
        ),
    )(
        source.reshape(4, 4, 4, 16, 128),
        coefficient.reshape(16, 128),
        orientation.reshape(6, 16, 128),
    )
    return out.reshape(4, 4, 4, 4, 4, 128)


def solution(mesh):
    in_specs = (
        P(None, None, None, "gx", "gy", "gz"),
        P("gx", "gy", "gz"),
        P(None, "gx", "gy", "gz"),
    )
    out_specs = P(None, None, None, "gx", "gy", "gz")
    return jax.shard_map(local, mesh=mesh, in_specs=in_specs, out_specs=out_specs, check_vma=False)
```

```python
import math

import jax
import jax.numpy as jnp
import numpy as np
from jax import lax
from jax.experimental import pallas as pl
from jax.experimental.pallas import tpu as pltpu
from jax.sharding import PartitionSpec as P

LOC = 2
TAU = 6.0
SHIFT = 1.0
OMEGA = 0.8
KEEP = 0.2
MESH = pl.DeviceIdType.MESH
F32 = jnp.float32


def lagrange(points, node_points):
    table = np.ones((points.shape[0], 4))
    for column in range(4):
        for other in range(4):
            if other != column:
                table[:, column] *= (points - node_points[other]) / (
                    node_points[column] - node_points[other]
                )
    return table


def jacobi_eigen(matrix):
    current = matrix.copy()
    vectors = np.eye(4)
    for sweep in range(12):
        for first in range(3):
            for second in range(first + 1, 4):
                angle = 0.5 * math.atan2(
                    2.0 * current[first, second], current[second, second] - current[first, first]
                )
                cosine = math.cos(angle)
                sine = math.sin(angle)
                rotation = np.eye(4)
                rotation[first, first] = cosine
                rotation[second, second] = cosine
                rotation[first, second] = sine
                rotation[second, first] = -sine
                current = rotation.T @ current @ rotation
                vectors = vectors @ rotation
    return (np.array([current[index, index] for index in range(4)]), vectors)


def tables():
    node_points = np.array([-1.0, -1.0 / math.sqrt(5.0), 1.0 / math.sqrt(5.0), 1.0])
    weights = np.array([1.0, 5.0, 5.0, 1.0]) / 6.0
    derivative = np.zeros((4, 4))
    for column in range(4):
        for other in range(4):
            if other != column:
                term = np.full(4, 1.0 / (node_points[column] - node_points[other]))
                for third in range(4):
                    if third != column and third != other:
                        term = (
                            term
                            * (node_points - node_points[third])
                            / (node_points[column] - node_points[third])
                        )
                derivative[:, column] += term
    stiffness = derivative.T @ (weights[:, None] * derivative)
    stiffness[0, 0] += TAU
    stiffness[3, 3] += TAU
    scale = weights ** (-0.5)
    eigen_values, eigen_vectors = jacobi_eigen(scale[:, None] * stiffness * scale[None, :])
    modes = scale[:, None] * eigen_vectors
    order = sorted(range(4), key=lambda mode: eigen_values[mode])
    eigen_values, modes = (eigen_values[order], modes[:, order])
    child = lagrange((node_points - 1.0) / 2.0, node_points)
    transfer = modes.T @ (weights[:, None] * (child @ modes))
    return (eigen_values, modes, transfer)


LAM, MODES, TRANSFER = tables()
PAR = (1.0, -1.0, 1.0, -1.0)
SIG = MODES[0]
SQ = [float(value * value) for value in SIG]
INTO = SIG[:, None] * MODES.T
MID = [float(MODES[1, mode] / SIG[mode]) for mode in range(4)]
REST = SIG[:, None] * TRANSFER.T / SIG[None, :]
EXT = SIG[:, None] * TRANSFER / SIG[None, :]


def level_scales(level):
    size_x = 2.0**level
    size_y = 2.0 ** min(level, LOC)
    return (size_y * size_y / size_x, size_x, size_x, size_x * size_y * size_y)


def roll(value, shift, axis):
    size = value.shape[axis]
    shift = shift % size
    if shift == 0:
        return value
    return pltpu.roll(value, shift, axis % value.ndim)


def iota(shape, axis):
    return lax.broadcasted_iota(jnp.int32, shape, axis)


def combine(row, parts):
    total = None
    for factor, part in zip(row, parts):
        term = part * float(factor)
        total = term if total is None else total + term
    return total


def into_modes(s0, s1, s2, s3):
    e0, e1, o0, o1 = (s0 + s3, s1 + s2, s0 - s3, s1 - s2)
    return [
        combine((INTO[mode, 0], INTO[mode, 1]), (e0, e1) if PAR[mode] > 0 else (o0, o1))
        for mode in range(4)
    ]


def from_modes(x0, x1, x2, x3):
    even, odd = (x0 + x2, x1 + x3)
    inner_even = x0 * MID[0] + x2 * MID[2]
    inner_odd = x1 * MID[1] + x3 * MID[3]
    return [even + odd, inner_even + inner_odd, inner_even - inner_odd, even - odd]


def restrict4(first, second):
    plus = [a + b for a, b in zip(first, second)]
    minus = [a - b for a, b in zip(first, second)]
    even = (plus[0], minus[1], plus[2], minus[3])
    odd = (minus[0], plus[1], minus[2], plus[3])
    return [combine(REST[mode], even if PAR[mode] > 0 else odd) for mode in range(4)]


def extend4(parts, sign):
    x0, x1, x2, x3 = parts
    out = []
    for mode in range(4):
        same, other = ((x0, x2), (x1, x3))
        row_same, row_other = ((EXT[mode, 0], EXT[mode, 2]), (EXT[mode, 1], EXT[mode, 3]))
        if PAR[mode] < 0:
            same, other, row_same, row_other = (other, same, row_other, row_same)
        out.append(combine(row_same, same) + sign * combine(row_other, other))
    return out


def extend4_mirrored(parts, sign):
    x0, x1, x2, x3 = parts
    one, two = ([], [])
    for mode in range(4):
        same, other = ((x0, x2), (x1, x3))
        row_same, row_other = ((EXT[mode, 0], EXT[mode, 2]), (EXT[mode, 1], EXT[mode, 3]))
        if PAR[mode] < 0:
            same, other, row_same, row_other = (other, same, row_other, row_same)
        a, b = (combine(row_same, same), sign * combine(row_other, other))
        one.append(a + b)
        two.append(a - b)
    return one, two


def extend4_pair(parts):
    x0, x1, x2, x3 = parts
    low, high = ([], [])
    for mode in range(4):
        same, other = ((x0, x2), (x1, x3))
        row_same, row_other = ((EXT[mode, 0], EXT[mode, 2]), (EXT[mode, 1], EXT[mode, 3]))
        if PAR[mode] < 0:
            same, other, row_same, row_other = (other, same, row_other, row_same)
        a, b = (combine(row_same, same), combine(row_other, other))
        low.append(a + b)
        high.append(a - b)
    return low, high


def inverse_tables(g_ref, d_ref, coefficient, level):
    wide_x, wide_y, wide_z, volume = level_scales(level)
    done = {}
    for i in range(4):
        for j in range(4):
            for k in range(4):
                key = (i,) + tuple(sorted((j, k)))
                if wide_x == wide_y:
                    key = tuple(sorted((i, j, k)))
                if key not in done:
                    spectrum = float(wide_x * LAM[i] + wide_y * LAM[j] + wide_z * LAM[k])
                    diagonal = coefficient * spectrum + SHIFT * volume
                    done[key] = (OMEGA / diagonal, diagonal)
                g_ref[i, j, k] = done[key][0]
                d_ref[i, j, k] = done[key][1]


def first_guess(x_ref, b_ref, g_ref):
    for i in range(4):
        for j in range(4):
            x_ref[i, j] = g_ref[i, j] * b_ref[i, j]


def face_pair(x_ref, axis, line):
    if axis == 0:
        parts = [x_ref[mode, line] for mode in range(4)]
    elif axis == 1:
        parts = [x_ref[line, mode] for mode in range(4)]
    else:
        parts = [x_ref[line, :, mode] for mode in range(4)]
    even, odd = (parts[0] + parts[2], parts[1] + parts[3])
    return even + odd, even - odd


def neighbours(f_ref, i, j):
    along_z = [f_ref[2, k % 2, i, j] * SQ[k] for k in range(4)]
    return f_ref[1, j % 2, i] * SQ[j] + jnp.stack(along_z, axis=0)


def flux_yz(b_ref, f_ref, i, j):
    return b_ref[i, j] + neighbours(f_ref, i, j)


def flux(b_ref, f_ref, i, j):
    return flux_yz(b_ref, f_ref, i, j) + f_ref[0, i % 2, j] * SQ[i]


def sweep(x_ref, b_ref, g_ref, f_ref):
    for i in range(4):
        for j in range(4):
            x_ref[i, j] = x_ref[i, j] * KEEP + g_ref[i, j] * flux(b_ref, f_ref, i, j)


def residual(r_ref, x_ref, b_ref, d_ref, f_ref):
    for i in range(4):
        for j in range(4):
            r_ref[i, j] = flux(b_ref, f_ref, i, j) - d_ref[i, j] * x_ref[i, j]


class Halo:
    def __init__(self, rows, stride, x, b, g, d, r, t, f, coefficient, wide, orientation, signs):
        self.rows, self.stride = (rows, stride)
        self.x, self.b, self.g, self.d, self.r, self.t, self.f = (x, b, g, d, r, t, f)
        self.coefficient, self.wide = (coefficient, wide)
        self.orientation, self.signs = (orientation, signs)

    def send(self, link):
        rows, stride = (self.rows, self.stride)
        low_rows = iota((4, 8, 128), 1) < 4
        lane = iota((rows, 128), 1)
        firsts, lasts = ([], [])
        for j in range(4):
            low, high = face_pair(self.x, 0, j)
            up, down = (roll(high, 4, 1), roll(low, rows - 4, 1))
            self.t[0, 0, j] = up
            self.t[0, 1, j] = down
            firsts.append((up[:, :8], low[:, :8]))
            lasts.append((high[:, rows - 8 :], down[:, rows - 8 :]))
        for j in range(2):
            link.px[0, j] = jnp.where(low_rows, firsts[j][0], lasts[j + 2][0])
            link.px[1, j] = jnp.where(low_rows, firsts[j][1], lasts[j + 2][1])
        link.start_x()
        packed_high = packed_low = jnp.zeros((rows, 128), F32)
        for i in range(4):
            low, high = face_pair(self.x, 2, i)
            self.t[2, 0, i] = roll(high, stride, 2)
            self.t[2, 1, i] = roll(low, 128 - stride, 2)
            for j in range(4):
                spot = 4 * i + j
                packed_high = jnp.where(lane == spot, roll(high[j], spot + stride, 1), packed_high)
                packed_low = jnp.where(lane == spot, roll(low[j], spot, 1), packed_low)
        link.pz[0] = packed_high
        link.pz[1] = packed_low
        link.start_z()
        for i in range(4):
            low, high = face_pair(self.x, 1, i)
            self.t[1, 0, i] = roll(high, stride, 1)
            self.t[1, 1, i] = roll(low, rows - stride, 1)
            link.py[0, i] = high
            link.py[1, i] = low
        link.start_y()

    def merge(self, axis):
        for line, even, odd in self.merged(axis):
            self.f[axis, 0, line] = even
            self.f[axis, 1, line] = odd

    def merged(self, axis):
        rows = self.rows
        factor = (TAU * self.wide * self.coefficient[...])[None]
        for line in range(4):
            pair = []
            for side in range(2):
                value = self.t[axis, side, line]
                if self.orientation is not None:
                    face = 2 * axis + side
                    swap = jnp.broadcast_to(self.orientation[face][None], (4, rows, 128)) % 2 == 1
                    value = jnp.where(swap, self.t[axis, side, :, line], value)
                    value = value * self.signs[face, line % 2]
                pair.append(value)
            yield line, factor * (pair[0] + pair[1]), factor * (pair[0] - pair[1])

    def land_y(self, link):
        rows, stride = (self.rows, self.stride)
        link.wait_y()
        inner = iota((4, rows, 128), 1) % 4
        back = 4 - stride
        for i in range(4):
            self.t[1, 0, i] = jnp.where(inner == 0, roll(link.qy[0, i], rows - back, 1), self.t[1, 0, i])
            self.t[1, 1, i] = jnp.where(inner == back, roll(link.qy[1, i], back, 1), self.t[1, 1, i])

    def land_z(self, link):
        rows, stride = (self.rows, self.stride)
        link.wait_z()
        lane = iota((rows, 128), 1)
        high, low = (link.qz[0], link.qz[1])
        for i in range(4):
            for j in range(4):
                spot = 4 * i + j
                self.t[2, 0, i, j] = jnp.where(lane == 0, roll(high, 128 - spot, 1), self.t[2, 0, i, j])
                self.t[2, 1, i, j] = jnp.where(
                    lane == 128 - stride, roll(low, 128 - stride - spot, 1), self.t[2, 1, i, j]
                )

    def land_x(self, link):
        rows = self.rows
        link.wait_x()
        low_rows = iota((4, 8, 128), 1) < 4
        for j in range(4):
            high, low = (link.qx[0, j % 2], link.qx[1, j % 2])
            if j < 2:
                low = roll(low, 4, 1)
            else:
                high = roll(high, 4, 1)
            self.t[0, 0, j, :, :8] = jnp.where(low_rows, high, self.t[0, 0, j, :, :8])
            self.t[0, 1, j, :, rows - 8 :] = jnp.where(low_rows, self.t[0, 1, j, :, rows - 8 :], low)

    def receive(self, link, defect, between=None):
        self.land_y(link)
        self.merge(1)
        self.land_z(link)
        self.merge(2)
        for i in range(4):
            for j in range(4):
                add = flux_yz(self.b, self.f, i, j)
                if defect:
                    self.r[i, j] = add - self.d[i, j] * self.x[i, j]
                else:
                    self.x[i, j] = self.x[i, j] * KEEP + self.g[i, j] * add
        if between is not None:
            between()
        self.land_x(link)
        for j, even, odd in self.merged(0):
            for i in range(4):
                add = (even if i % 2 == 0 else odd) * SQ[i]
                if defect:
                    self.r[i, j] += add
                else:
                    self.x[i, j] += self.g[i, j] * add

    def correct(self, change, halo):
        rows, stride = (self.rows, self.stride)
        row, lane = (iota((4, rows, 128), 1), iota((4, rows, 128), 2))
        low_rows = iota((4, 8, 128), 1) < 4
        for line in range(4):
            low, high = face_pair(change, 0, line)
            up, down = (roll(high, 4, 1), roll(low, rows - 4, 1))
            beyond = halo[0, line, :, :8]
            self.t[0, 0, line] = up
            self.t[0, 1, line] = down
            self.t[0, 0, line, :, :8] = jnp.where(low_rows, beyond, up[:, :8])
            self.t[0, 1, line, :, rows - 8 :] = jnp.where(low_rows, down[:, rows - 8 :], beyond)
            low, high = face_pair(change, 1, line)
            beyond = halo[1, line]
            self.t[1, 0, line] = jnp.where(row % 4 == 0, beyond, roll(high, stride, 1))
            self.t[1, 1, line] = jnp.where(row % 4 == 4 - stride, beyond, roll(low, rows - stride, 1))
            low, high = face_pair(change, 2, line)
            beyond = halo[2, line]
            self.t[2, 0, line] = jnp.where(lane == 0, beyond, roll(high, stride, 2))
            self.t[2, 1, line] = jnp.where(lane == 128 - stride, beyond, roll(low, 128 - stride, 2))
        for axis in range(3):
            self.merge(axis)
        for i in range(4):
            for j in range(4):
                add = neighbours(self.f, i, j) + self.f[0, i % 2, j] * SQ[i]
                self.x[i, j] += change[i, j] * KEEP + self.g[i, j] * add


class Link:
    def __init__(self, px, qx, py, qy, pz, qz, send, recv, at):
        self.px, self.qx, self.py, self.qy, self.pz, self.qz = (px, qx, py, qy, pz, qz)
        gx, gy, gz = at

        def copy(src, dst, spot, device):
            return pltpu.make_async_remote_copy(
                src_ref=src,
                dst_ref=dst,
                send_sem=send.at[spot],
                recv_sem=recv.at[spot],
                device_id=device,
                device_id_type=MESH,
            )

        self.x_copies = [
            copy(px.at[0], qx.at[0], 0, {"gx": lax.rem(gx + 1, 32)}),
            copy(px.at[1], qx.at[1], 1, {"gx": lax.rem(gx + 31, 32)}),
        ]
        self.z_copies = [
            copy(pz.at[0], qz.at[0], 2, {"gz": lax.rem(gz + 1, 4)}),
            copy(pz.at[1], qz.at[1], 3, {"gz": lax.rem(gz + 3, 4)}),
        ]
        self.y_copies = [copy(py, qy, 4, {"gy": 1 - gy})]

    def start_x(self):
        for item in self.x_copies:
            item.start()

    def start_y(self):
        for item in self.y_copies:
            item.start()

    def start_z(self):
        for item in self.z_copies:
            item.start()

    def wait_x(self):
        for item in self.x_copies:
            item.wait_recv()

    def wait_y(self):
        for item in self.y_copies:
            item.wait_recv()

    def wait_z(self):
        for item in self.z_copies:
            item.wait_recv()

    def close(self):
        for item in self.x_copies + self.y_copies + self.z_copies:
            item.wait_send()


class Whole:
    def __init__(self, level, count, x, b, g, d, r, f, coefficient):
        self.level, self.count = (level, count)
        self.x, self.b, self.g, self.d, self.r, self.f = (x, b, g, d, r, f)
        self.coefficient = coefficient

    def faces(self):
        wide_x, wide_y, wide_z, _ = level_scales(self.level)
        count = self.count
        coefficient = self.coefficient[...][None]
        ends = iota((4, count, 8, 128), 3) % 64
        for line in range(4):
            low, high = face_pair(self.x, 0, line)
            before, after = (roll(high[:, count - 1 :], 1, 2), roll(low[:, :1], 7, 2))
            if count > 1:
                before = jnp.concatenate([before, high[:, : count - 1]], axis=1)
                after = jnp.concatenate([low[:, 1:], after], axis=1)
            factor = coefficient * (TAU * wide_x)
            self.f[0, 0, line] = factor * (before + after)
            self.f[0, 1, line] = factor * (before - after)
            low, high = face_pair(self.x, 1, line)
            factor = coefficient * (TAU * wide_y)
            self.f[1, 0, line] = factor * roll(high + low, 64, 3)
            self.f[1, 1, line] = factor * roll(high - low, 64, 3)
            low, high = face_pair(self.x, 2, line)
            factor = coefficient * (TAU * wide_z)
            before = jnp.where(ends < 4, roll(high, 69, 3), roll(high, 4, 3))
            after = jnp.where(ends >= 60, roll(low, 59, 3), roll(low, 124, 3))
            self.f[2, 0, line] = factor * (before + after)
            self.f[2, 1, line] = factor * (before - after)

    def tables(self):
        inverse_tables(self.g, self.d, self.coefficient[...], self.level)

    def before(self):
        first_guess(self.x, self.b, self.g)
        self.faces()
        sweep(self.x, self.b, self.g, self.f)

    def down(self, coarse):
        self.faces()
        residual(self.r, self.x, self.b, self.d, self.f)
        for j in range(4):
            for block in range(coarse.count):
                first = [self.r[i, j, :, 2 * block] for i in range(4)]
                second = [self.r[i, j, :, 2 * block + 1] for i in range(4)]
                for i, value in enumerate(restrict4(first, second)):
                    coarse.b[i, j, :, block] = value

    def up(self, coarse):
        for j in range(4):
            for block in range(coarse.count):
                low, high = extend4_pair([coarse.x[i, j, :, block] for i in range(4)])
                for i in range(4):
                    self.x[i, j, :, 2 * block] += low[i]
                    self.x[i, j, :, 2 * block + 1] += high[i]
        for step in range(2):
            self.faces()
            sweep(self.x, self.b, self.g, self.f)


class Beyond:
    def __init__(self, e, g, f, h, coefficient):
        self.e, self.g, self.f, self.h, self.coefficient = (e, g, f, h, coefficient)

    def smooth(self, count, beyond):
        factor = (TAU * level_scales(1)[0]) * self.coefficient[:count][None]
        low_rows = iota((4, 8, 128), 1) < 4
        row, lane = (iota((4, count, 8, 128), 2) % 4, iota((4, count, 8, 128), 3))
        for line in range(4):
            low, high = face_pair(self.e, 0, line)
            ha, hb, hc = (high[:, block] for block in range(3))
            la, lb, lc = (low[:, block] for block in range(3))
            far = self.h[line] if beyond else hc
            ta, sa = (roll(ha, 4, 1), roll(la, 4, 1))
            before = [jnp.where(low_rows, roll(hb, 4, 1), ta), jnp.where(low_rows, ta, hc), jnp.where(low_rows, hb, far)]
            after = [jnp.where(low_rows, sa, roll(lb, 4, 1)), jnp.where(low_rows, lc, sa), jnp.where(low_rows, far, lb)]
            before, after = (jnp.stack(before[:count], axis=1), jnp.stack(after[:count], axis=1))
            self.f[0, 0, line, :, :count] = factor * (before + after)
            self.f[0, 1, line, :, :count] = factor * (before - after)
            low, high = face_pair(self.e, 1, line)
            low, high = (low[:, :count], high[:, :count])
            before = jnp.where(row == 0, roll(high, 5, 2), roll(high, 1, 2))
            after = jnp.where(row == 3, roll(low, 3, 2), roll(low, 7, 2))
            self.f[1, 0, line, :, :count] = factor * (before + after)
            self.f[1, 1, line, :, :count] = factor * (before - after)
            low, high = face_pair(self.e, 2, line)
            low, high = (low[:, :count], high[:, :count])
            before = jnp.where(lane == 0, roll(high, 1, 3), jnp.where(lane == 1, roll(high, 3, 3), roll(high, 2, 3)))
            after = jnp.where(
                lane == 126, roll(low, 125, 3), jnp.where(lane == 127, roll(low, 127, 3), roll(low, 126, 3))
            )
            self.f[2, 0, line, :, :count] = factor * (before + after)
            self.f[2, 1, line, :, :count] = factor * (before - after)
        for i in range(4):
            for j in range(4):
                along_z = [self.f[2, k % 2, i, j, :count] * SQ[k] for k in range(4)]
                add = jnp.stack(along_z, axis=0) + self.f[1, j % 2, i, :, :count] * SQ[j]
                add = add + self.f[0, i % 2, j, :, :count] * SQ[i]
                self.e[i, j, :, :count] = self.e[i, j, :, :count] * KEEP + self.g[i, j, :, :count] * add


def kernel(
    source_in,
    coefficient_in,
    orientation_in,
    out,
    source, coefficient, orientation, input_sem,
    x0, b0, g0, d0, r0, t0, f0, signs,
    x1, b1, g1, d1, r1, t1, f1, c1, w1, v1,
    x2, b2, g2, d2, r2, f2, c2,
    x3, b3, g3, d3, r3, f3, c3,
    x4, b4, g4, d4, r4, f4, c4,
    px, qx, py0, qy0, pz0, qz0, py1, qy1, pz1, qz1,
    cs, call, cown, cin,
    ms, mall, my, mz,
    face_send, face_recv,
    c_send, c_recv, c_send2, c_recv2,
    m_send, m_recv, m_send2, m_recv2,
    told,
    e1, ge, fe, he, ce, de, halo1, halo0, wb,
    near_y, near_z, near_x, near_send, near_recv, spare,
):
    inputs = [
        pltpu.make_async_copy(src, dst, input_sem.at[spot])
        for spot, (src, dst) in enumerate(
            ((coefficient_in, coefficient), (source_in, source), (orientation_in, orientation))
        )
    ]
    for item in inputs:
        item.start()
    gx, gy, gz = (lax.axis_index("gx"), lax.axis_index("gy"), lax.axis_index("gz"))
    slow, fast = (gx // 4, lax.rem(gx, 4))
    slow_at = pl.multiple_of(slow * 16, 16)
    slow_at8 = pl.multiple_of(slow * 8, 8)
    offsets = [(a, b) for a in range(8) for b in range(4) if (a, b) != (0, 0)]

    def along_x(a, b):
        return {"gx": lax.rem(slow + a, 8) * 4 + lax.rem(fast + b, 4)}

    def beside(step):
        return {"gx": lax.rem(gx + step + 32, 32)}

    up_z, down_z = (lax.rem(gz + 1, 4), lax.rem(gz + 3, 4))
    around = [
        {"gy": 1 - gy},
        {"gz": up_z},
        {"gy": 1 - gy, "gz": up_z},
        {"gz": down_z},
        {"gy": 1 - gy, "gz": down_z},
    ]

    barrier = pltpu.get_barrier_semaphore()
    for device in (beside(1), beside(-1), {"gy": 1 - gy}, {"gz": up_z}, {"gz": down_z}):
        pl.semaphore_signal(barrier, inc=1, device_id=device, device_id_type=MESH)

    for item in inputs:
        item.wait()
    for i in range(4):
        for k, value in enumerate(into_modes(*[source[i, :, k] for k in range(4)])):
            b0[i, :, k] = value
    for i in range(4):
        for j, value in enumerate(into_modes(*[b0[i, j] for j in range(4)])):
            b0[i, j] = value
    for j in range(4):
        for i, value in enumerate(into_modes(*[b0[i, j] for i in range(4)])):
            b0[i, j] = value
    inverse_tables(g0, d0, coefficient[...], 0)
    first_guess(x0, b0, g0)
    for face in range(6):
        code = orientation[face]
        one = jnp.ones((16, 128), F32)
        first = jnp.where(code // 2 % 2 == 1, -one, one)
        second = jnp.where(code // 4 == 1, -one, one)
        signs[face, 0] = jnp.stack([one, second, one, second], axis=0)
        signs[face, 1] = jnp.stack([first, first * second, first, first * second], axis=0)

    row8 = iota((8, 128), 0)
    lane8 = iota((8, 128), 1)
    top, bottom = (coefficient[:8], coefficient[8:])
    value = 0.5 * (
        jnp.where(row8 < 4, top, roll(bottom, 4, 0)) + jnp.where(row8 < 4, roll(top, 4, 0), bottom)
    )
    value = 0.5 * (value + roll(value, 7, 0))
    value = 0.5 * (value + roll(value, 127, 1))
    c1[...] = value
    inverse_tables(g1, d1, value, 1)
    value = 0.5 * (value + roll(value, 4, 0))
    value = 0.5 * (value + roll(value, 6, 0))
    cs[...] = 0.5 * (value + roll(value, 126, 1))

    pl.semaphore_wait(barrier, 5)

    def tell(step):
        devices = [beside(2**step), beside(-(2**step))]
        if step == 0:
            devices.append({"gy": 1 - gy})
        for device in devices:
            pl.semaphore_signal(told.at[step], inc=1, device_id=device, device_id_type=MESH)

    def heard(step):
        pl.semaphore_wait(told.at[step], 3 if step == 0 else 2)
        if step < 3:
            tell(step + 1)

    tell(0)

    def link(level, step):
        spot = 4 * level + step
        py, qy, pz, qz = (py0, qy0, pz0, qz0) if level == 0 else (py1, qy1, pz1, qz1)
        return Link(
            px.at[spot], qx.at[spot], py.at[step], qy.at[step], pz.at[step], qz.at[step],
            face_send.at[spot], face_recv.at[spot], (gx, gy, gz),
        )

    def copy(src, dst, send, recv, device):
        return pltpu.make_async_remote_copy(
            src_ref=src, dst_ref=dst, send_sem=send, recv_sem=recv, device_id=device, device_id_type=MESH
        )

    fine = Halo(16, 1, x0, b0, g0, d0, r0, t0, f0, coefficient, 1.0, orientation, signs)
    mid = Halo(8, 2, x1, b1, g1, d1, r1, t1, f1, c1, 2.0, None, None)
    links = []

    near_copies = [copy(c1, near_y, near_send.at[0], near_recv.at[0], {"gy": 1 - gy})]
    near_copies[0].start()
    ring = iota((8, 128), 0) % 4

    def near_step(step):
        if step == 0:
            near_copies[0].wait_recv()
            own, other = (c1[...], near_y[...])
            value = jnp.where(ring < 2, jnp.where(ring == 0, own, roll(own, 7, 0)),
                              jnp.where(ring == 2, roll(other, 2, 0), roll(other, 1, 0)))
            spare[0] = value
            for spot, device in ((1, {"gz": down_z}), (2, {"gz": up_z})):
                item = copy(spare.at[0], near_z.at[spot - 1], near_send.at[spot], near_recv.at[spot], device)
                item.start()
                near_copies.append(item)
        elif step == 1:
            near_copies[1].wait_recv()
            near_copies[2].wait_recv()
            outer = jnp.where(lane8 < 64, roll(near_z[0], 1, 1), roll(near_z[1], 1, 1))
            value = jnp.where(lane8 % 2 == 0, spare[0], outer)
            spare[1] = value
            ce[0] = value
            for spot, device in ((3, beside(-1)), (4, beside(1))):
                item = copy(spare.at[1], near_x.at[spot - 3], near_send.at[spot], near_recv.at[spot], device)
                item.start()
                near_copies.append(item)
        else:
            near_copies[3].wait_recv()
            near_copies[4].wait_recv()
            after, before = (near_x[0], near_x[1])
            ce[1] = jnp.where(row8 < 4, after, before)
            ce[2] = jnp.where(row8 < 4, roll(after, 4, 0), roll(before, 4, 0))
            inverse_tables(ge, de, ce[...], 1)

    links.append(link(0, 0))
    fine.send(links[-1])
    fine.receive(links[-1], False, lambda: (heard(0), near_step(0)))
    links.append(link(0, 1))
    fine.send(links[-1])
    fine.receive(links[-1], True, lambda: (heard(1), near_step(1)))
    row4 = iota((4, 8, 128), 1)
    lane4 = iota((4, 8, 128), 2)
    for j in range(4):
        first, second = ([], [])
        for i in range(4):
            top, bottom = (r0[i, j, :, :8], r0[i, j, :, 8:])
            first.append(jnp.where(row4 < 4, top, roll(bottom, 4, 1)))
            second.append(jnp.where(row4 < 4, roll(top, 4, 1), bottom))
        for i, value in enumerate(restrict4(first, second)):
            w1[i, j] = value
    for i in range(4):
        first = [w1[i, j] for j in range(4)]
        for j, value in enumerate(restrict4(first, [roll(item, 7, 1) for item in first])):
            v1[i, j] = value
    for i in range(4):
        first = [v1[i, :, k] for k in range(4)]
        for k, value in enumerate(restrict4(first, [roll(item, 127, 2) for item in first])):
            b1[i, :, k] = value

    first_guess(x1, b1, g1)
    links.append(link(1, 0))
    mid.send(links[-1])
    mid.receive(links[-1], False, lambda: (heard(2), near_step(2)))
    links.append(link(1, 1))
    mid.send(links[-1])
    c_copies = [
        copy(cs, call.at[fast, pl.ds(slow_at8, 8)], c_send.at[a, b], c_recv.at[a, b], along_x(a, b))
        for a, b in offsets
    ]

    def send_coefficients():
        heard(3)
        for item in c_copies:
            item.start()
        call[fast, pl.ds(slow_at8, 8), :] = cs[...]

    mid.receive(links[-1], True, send_coefficients)
    for j in range(4):
        first = [r1[i, j] for i in range(4)]
        for i, value in enumerate(restrict4(first, [roll(item, 4, 1) for item in first])):
            w1[i, j] = value
    for i in range(4):
        first = [w1[i, j] for j in range(4)]
        for j, value in enumerate(restrict4(first, [roll(item, 6, 1) for item in first])):
            v1[i, j] = value
    packed = []
    for i in range(4):
        first = [v1[i, :, k] for k in range(4)]
        total = None
        for k, value in enumerate(restrict4(first, [roll(item, 126, 2) for item in first])):
            total = value if k == 0 else jnp.where(lane4 % 4 == k, roll(value, k, 2), total)
        packed += [total[j] for j in range(4)]
    for line in range(8):
        low, high = (packed[line], packed[line + 8])
        ms[pl.ds(line, 1), :] = jnp.where(lane8 < 64, low, roll(high, 64, 1))[:1]
        ms[pl.ds(line + 8, 1), :] = jnp.where(lane8 < 64, roll(low, 64, 1), high)[:1]

    m_copies = {
        (a, b): copy(ms, mall.at[fast, pl.ds(slow_at, 16)], m_send.at[a, b], m_recv.at[a, b], along_x(a, b))
        for a, b in offsets
    }
    for item in m_copies.values():
        item.start()
    mall[fast, pl.ds(slow_at, 16), :] = ms[...]
    for item in c_copies:
        item.wait_recv()
    for block in range(4):
        cown[block] = call[block, pl.ds(0, 8, stride=8), :]
    c_around = [
        copy(cown, cin.at[spot], c_send2.at[spot], c_recv2.at[spot], device)
        for spot, device in enumerate(around)
    ]
    for item in c_around:
        item.start()
    for i in range(4):
        for j in range(4):
            x1[i, j] += g1[i, j] * r1[i, j]
    links.append(link(1, 2))
    mid.send(links[-1])
    passed = []
    for a in range(8):
        for b in range(4):
            if (a, b) != (0, 0):
                m_copies[a, b].wait_recv()
        start = lax.rem(slow + 8 - a, 8)
        start16 = pl.multiple_of(start * 16, 16)
        start8 = pl.multiple_of(start * 8, 8)
        upper = pl.multiple_of(start * 16 + 8, 8)
        for spot, device in enumerate(around):
            if spot == 0:
                src, dst = (mall.at[:, pl.ds(start16, 16)], my.at[:, pl.ds(start16, 16)])
            else:
                src = mall.at[:, pl.ds(upper if spot < 3 else start16, 8)]
                dst = mz.at[spot - 1, :, pl.ds(start8, 8)]
            item = copy(src, dst, m_send2.at[spot, a], m_recv2.at[spot, a], device)
            item.start()
            passed.append(item)
    for item in c_around:
        item.wait_recv()
    for block in range(4):
        mine, other = (cown[block], cin[0, block])
        below, below_other, above, above_other = (cin[spot, block] for spot in range(1, 5))
        phase = lane8 % 4
        near = jnp.where(phase == 0, roll(below, 64, 1), roll(mine, 1, 1))
        near = jnp.where(phase == 2, roll(mine, 66, 1), near)
        near = jnp.where(phase == 3, roll(above, 3, 1), near)
        far = jnp.where(phase == 0, below_other, roll(other, 65, 1))
        far = jnp.where(phase == 2, roll(other, 2, 1), far)
        far = jnp.where(phase == 3, roll(above_other, 67, 1), far)
        c2[block] = jnp.where(lane8 < 64, near, far)
    for block in range(2):
        c3[block] = 0.5 * (c2[2 * block] + c2[2 * block + 1])
    c4[0] = 0.5 * (c3[0] + c3[1])
    level2 = Whole(2, 4, x2, b2, g2, d2, r2, f2, c2)
    level3 = Whole(3, 2, x3, b3, g3, d3, r3, f3, c3)
    level4 = Whole(4, 1, x4, b4, g4, d4, r4, f4, c4)
    for level in (level2, level3, level4):
        level.tables()
    mid.receive(links[-1], False)
    links.append(link(1, 3))
    mid.send(links[-1])
    for i in range(4):
        for j in range(4):
            x0[i, j] += g0[i, j] * r0[i, j]
    for item in passed:
        item.wait_recv()

    def unpack(block, carry):
        odd, pair = (lane8 % 2 == 1, lane8 % 4 >= 2)
        for line in range(8):
            def rows(ref, start, stride):
                return ref[block, pl.ds(start, 8, stride=stride), :]

            near = [
                rows(mz.at[0], line, 8), rows(mall, line, 16), rows(mall, line + 8, 16), rows(mz.at[2], line, 8)
            ]
            far = [
                rows(mz.at[1], line, 8), rows(my, line, 16), rows(my, line + 8, 16), rows(mz.at[3], line, 8)
            ]
            for half in range(2):
                if half == 0:
                    part = [jnp.where(lane8 < 64, a, roll(b, 64, 1)) for a, b in zip(near, far)]
                else:
                    part = [jnp.where(lane8 < 64, roll(a, 64, 1), b) for a, b in zip(near, far)]
                step = [
                    jnp.where(odd, roll(part[1], 1, 1), part[0]),
                    jnp.where(odd, part[1], roll(part[0], 127, 1)),
                    jnp.where(odd, roll(part[3], 1, 1), part[2]),
                    jnp.where(odd, part[3], roll(part[2], 127, 1)),
                ]
                last = [
                    jnp.where(pair, roll(step[2], 2, 1), step[0]),
                    jnp.where(pair, roll(step[3], 2, 1), step[1]),
                    jnp.where(pair, step[2], roll(step[0], 126, 1)),
                    jnp.where(pair, step[3], roll(step[1], 126, 1)),
                ]
                mode = line + 8 * half
                for k in range(4):
                    b2[mode // 4, mode % 4, k, block] = last[k]
        return carry

    lax.fori_loop(0, 4, unpack, 0)
    level2.before()
    level2.down(level3)
    level3.before()
    level3.down(level4)
    level4.before()
    level3.up(level4)
    level2.up(level3)

    def element(step):
        place = lax.rem(gx + step + 32, 32)
        return place // 4, lax.rem(place, 4)

    def take(i, j, step):
        at, block = element(step)
        return jnp.broadcast_to(x2[i, j, :, block, pl.ds(at, 1), :], (4, 8, 128))

    def spread(value):
        value = jnp.where(row4 % 4 < 2, value, roll(value, 64, 2))
        low = jnp.where(lane4 % 2 == 0, roll(value, 127, 2), roll(value, 126, 2))
        high = jnp.where(lane4 % 2 == 0, roll(value, 62, 2), roll(value, 65, 2))
        value = jnp.where(lane4 < 64, low, high)
        return jnp.where(lane4 % 4 < 2, value, roll(value, 2, 2))

    one = jnp.ones((4, 8, 128), F32)
    sign_z = jnp.where(lane4 % 4 < 2, one, -one)
    sign_y = jnp.where(row4 % 2 == 0, one, -one)
    sign_x = jnp.where(row4 < 4, one, -one)
    for i in range(4):
        for j in range(4):
            w1[i, j] = spread(take(i, j, 0))
            wb[i, j] = spread(jnp.where(row4 < 4, take(i, j, 1), take(i, j, -1)))
    for j in range(4):
        after = [take(i, j, 2) for i in range(4)]
        before = [take(i, j, -2) for i in range(4)]
        low = (after[0] + after[2]) + (after[1] + after[3])
        high = (before[0] + before[2]) - (before[1] + before[3])
        he[j] = spread(jnp.where(row4 < 4, low, high))
    for ref in (w1, wb):
        for i in range(4):
            for k, value in enumerate(extend4([ref[i, :, k] for k in range(4)], sign_z)):
                ref[i, :, k] = value
        for i in range(4):
            for j, value in enumerate(extend4([ref[i, j] for j in range(4)], sign_y)):
                ref[i, j] = value
    for k, value in enumerate(extend4([he[:, k] for k in range(4)], sign_z)):
        he[:, k] = value
    for j, value in enumerate(extend4([he[j] for j in range(4)], sign_y)):
        he[j] = value
    for j in range(4):
        for i, value in enumerate(extend4([w1[i, j] for i in range(4)], sign_x)):
            e1[i, j, :, 0] = value
        for i, (value, other) in enumerate(zip(*extend4_mirrored([wb[i, j] for i in range(4)], sign_x))):
            e1[i, j, :, 1] = value
            e1[i, j, :, 2] = other
    beyond = Beyond(e1, ge, fe, he, ce)
    beyond.smooth(3, True)
    beyond.smooth(2, False)

    mid.land_y(links[-1])
    mid.land_z(links[-1])
    mid.land_x(links[-1])

    def own_rows(value):
        return jnp.where(row4 % 4 == 2, roll(value, 1, 1), value)

    for line in range(4):
        parts = [e1[i, line, :, 1] for i in range(4)]
        even, odd = (parts[0] + parts[2], parts[1] + parts[3])
        value = own_rows(roll(jnp.where(row4 < 4, even + odd, even - odd), 4, 1))
        halo1[0, line] = value + jnp.where(row4 < 4, t1[0, 0, line], t1[0, 1, line])
        parts = [e1[line, j, :, 0] for j in range(4)]
        even, odd = (parts[0] + parts[2], parts[1] + parts[3])
        value = jnp.where(row4 % 4 == 0, roll(even - odd, 5, 1), even + odd)
        halo1[1, line] = value + jnp.where(row4 % 4 == 0, t1[1, 0, line], t1[1, 1, line])
        parts = [e1[line, :, k, 0] for k in range(4)]
        even, odd = (parts[0] + parts[2], parts[1] + parts[3])
        value = own_rows(jnp.where(lane4 < 64, roll(even - odd, 1, 2), roll(even + odd, 125, 2)))
        halo1[2, line] = value + jnp.where(lane4 < 64, t1[2, 0, line], t1[2, 1, line])

    def fill(value):
        value = jnp.where(row4 % 2 == 0, value, roll(value, 1, 1))
        return jnp.where(lane4 % 2 == 0, value, roll(value, 1, 2))

    def doubled(value):
        turned = roll(value, 4, 1)
        low, high = (jnp.where(row4 < 4, value, turned), jnp.where(row4 < 4, turned, value))
        return jnp.concatenate([low, high], axis=1)

    for i in range(4):
        for j in range(4):
            w1[i, j] = fill(x1[i, j] + own_rows(e1[i, j, :, 0]))
    for axis in range(3):
        for line in range(4):
            halo1[axis, line] = fill(halo1[axis, line])
    sign_z = jnp.where(lane4 % 2 == 0, one, -one)
    wide_one = jnp.ones((4, 16, 128), F32)
    sign_x = jnp.where(iota((4, 16, 128), 1) % 8 < 4, wide_one, -wide_one)
    for i in range(4):
        for k, value in enumerate(extend4([w1[i, :, k] for k in range(4)], sign_z)):
            w1[i, :, k] = value
    for i in range(4):
        for j, value in enumerate(extend4([w1[i, j] for j in range(4)], sign_y)):
            w1[i, j] = value
    for j in range(4):
        for i, value in enumerate(extend4([doubled(w1[i, j]) for i in range(4)], sign_x)):
            r0[i, j] = value
    for axis in range(2):
        for k, value in enumerate(extend4([halo1[axis, :, k] for k in range(4)], sign_z)):
            halo1[axis, :, k] = value
    for line, value in enumerate(extend4([halo1[0, line] for line in range(4)], sign_y)):
        halo0[0, line, :, :8] = value
    for line, value in enumerate(extend4([doubled(halo1[1, line]) for line in range(4)], sign_x)):
        halo0[1, line] = value
    for line, value in enumerate(extend4([halo1[2, :, line] for line in range(4)], sign_y)):
        halo1[2, :, line] = value
    for line, value in enumerate(extend4([doubled(halo1[2, line]) for line in range(4)], sign_x)):
        halo0[2, line] = value
    fine.correct(r0, halo0)
    links.append(link(0, 2))
    fine.send(links[-1])
    fine.receive(links[-1], False)

    for i in range(4):
        for k, value in enumerate(from_modes(*[x0[i, :, k] for k in range(4)])):
            out[i, :, k] = value
    for i in range(4):
        for j, value in enumerate(from_modes(*[out[i, j] for j in range(4)])):
            out[i, j] = value
    for j in range(4):
        for i, value in enumerate(from_modes(*[out[i, j] for i in range(4)])):
            out[i, j] = value

    for item in links:
        item.close()
    for item in near_copies + c_copies + c_around + list(m_copies.values()) + passed:
        item.wait_send()


def scratch():
    def mem(*shape):
        return pltpu.VMEM(shape, F32)

    modes = (4, 4, 4)
    dma = pltpu.SemaphoreType.DMA
    inputs = [mem(*modes, 16, 128), mem(16, 128), pltpu.VMEM((6, 16, 128), jnp.int32), dma((3,))]
    level0 = [mem(*modes, 16, 128)] * 5 + [
        mem(3, 2, 4, 4, 16, 128), mem(3, 2, 4, 4, 16, 128), mem(6, 2, 4, 16, 128)
    ]
    level1 = [mem(*modes, 8, 128)] * 5 + [
        mem(3, 2, 4, 4, 8, 128), mem(3, 2, 4, 4, 8, 128), mem(8, 128), mem(*modes, 8, 128), mem(*modes, 8, 128)
    ]
    whole = []
    for count in (4, 2, 1):
        whole += [mem(*modes, count, 8, 128)] * 5 + [mem(3, 2, 4, 4, count, 8, 128), mem(count, 8, 128)]
    faces = [
        mem(8, 2, 2, 4, 8, 128), mem(8, 2, 2, 4, 8, 128),
        mem(4, 2, 4, 4, 16, 128), mem(4, 2, 4, 4, 16, 128), mem(4, 2, 16, 128), mem(4, 2, 16, 128),
        mem(4, 2, 4, 4, 8, 128), mem(4, 2, 4, 4, 8, 128), mem(4, 2, 8, 128), mem(4, 2, 8, 128),
    ]
    gathered = [
        mem(8, 128), mem(4, 64, 128), mem(4, 8, 128), mem(5, 4, 8, 128),
        mem(16, 128), mem(4, 128, 128), mem(4, 128, 128), mem(4, 4, 64, 128),
    ]
    sems = [dma((8, 5)), dma((8, 5)), dma((8, 4)), dma((8, 4)), dma((5,)), dma((5,)),
            dma((8, 4)), dma((8, 4)), dma((5, 8)), dma((5, 8)),
            pltpu.SemaphoreType.REGULAR((4,))]
    extended = [
        mem(*modes, 3, 8, 128), mem(*modes, 3, 8, 128), mem(3, 2, 4, 4, 3, 8, 128), mem(4, 4, 8, 128),
        mem(3, 8, 128), mem(*modes, 3, 8, 128), mem(3, 4, 4, 8, 128), mem(3, 4, 4, 16, 128), mem(*modes, 8, 128),
        mem(8, 128), mem(2, 8, 128), mem(2, 8, 128), dma((5,)), dma((5,)), mem(2, 8, 128),
    ]
    return inputs + level0 + level1 + whole + faces + gathered + sems + extended


def local(source, coefficient, orientation):
    vmem = pl.BlockSpec(memory_space=pltpu.VMEM)
    out = pl.pallas_call(
        kernel,
        out_shape=jax.ShapeDtypeStruct((4, 4, 4, 16, 128), F32),
        in_specs=[pl.BlockSpec(memory_space=pl.ANY)] * 3,
        out_specs=vmem,
        scratch_shapes=scratch(),
        compiler_params=pltpu.CompilerParams(
            collective_id=0, has_side_effects=True, vmem_limit_bytes=44 * 1024 * 1024
        ),
    )(
        source.reshape(4, 4, 4, 16, 128),
        coefficient.reshape(16, 128),
        orientation.reshape(6, 16, 128),
    )
    return out.reshape(4, 4, 4, 4, 4, 128)


def solution(mesh):
    in_specs = (
        P(None, None, None, "gx", "gy", "gz"),
        P("gx", "gy", "gz"),
        P(None, "gx", "gy", "gz"),
    )
    out_specs = P(None, None, None, "gx", "gy", "gz")
    return jax.shard_map(local, mesh=mesh, in_specs=in_specs, out_specs=out_specs, check_vma=False)
```

```python
import math

import jax
import jax.numpy as jnp
import numpy as np
from jax import lax
from jax.experimental import pallas as pl
from jax.experimental.pallas import tpu as pltpu
from jax.sharding import PartitionSpec as P

LOC = 2
TAU = 6.0
SHIFT = 1.0
OMEGA = 0.8
KEEP = 0.2
MESH = pl.DeviceIdType.MESH
F32 = jnp.float32


def lagrange(points, node_points):
    table = np.ones((points.shape[0], 4))
    for column in range(4):
        for other in range(4):
            if other != column:
                table[:, column] *= (points - node_points[other]) / (
                    node_points[column] - node_points[other]
                )
    return table


def jacobi_eigen(matrix):
    current = matrix.copy()
    vectors = np.eye(4)
    for sweep in range(12):
        for first in range(3):
            for second in range(first + 1, 4):
                angle = 0.5 * math.atan2(
                    2.0 * current[first, second], current[second, second] - current[first, first]
                )
                cosine = math.cos(angle)
                sine = math.sin(angle)
                rotation = np.eye(4)
                rotation[first, first] = cosine
                rotation[second, second] = cosine
                rotation[first, second] = sine
                rotation[second, first] = -sine
                current = rotation.T @ current @ rotation
                vectors = vectors @ rotation
    return (np.array([current[index, index] for index in range(4)]), vectors)


def tables():
    node_points = np.array([-1.0, -1.0 / math.sqrt(5.0), 1.0 / math.sqrt(5.0), 1.0])
    weights = np.array([1.0, 5.0, 5.0, 1.0]) / 6.0
    derivative = np.zeros((4, 4))
    for column in range(4):
        for other in range(4):
            if other != column:
                term = np.full(4, 1.0 / (node_points[column] - node_points[other]))
                for third in range(4):
                    if third != column and third != other:
                        term = (
                            term
                            * (node_points - node_points[third])
                            / (node_points[column] - node_points[third])
                        )
                derivative[:, column] += term
    stiffness = derivative.T @ (weights[:, None] * derivative)
    stiffness[0, 0] += TAU
    stiffness[3, 3] += TAU
    scale = weights ** (-0.5)
    eigen_values, eigen_vectors = jacobi_eigen(scale[:, None] * stiffness * scale[None, :])
    modes = scale[:, None] * eigen_vectors
    order = sorted(range(4), key=lambda mode: eigen_values[mode])
    eigen_values, modes = (eigen_values[order], modes[:, order])
    child = lagrange((node_points - 1.0) / 2.0, node_points)
    transfer = modes.T @ (weights[:, None] * (child @ modes))
    return (eigen_values, modes, transfer)


LAM, MODES, TRANSFER = tables()
PAR = (1.0, -1.0, 1.0, -1.0)
SIG = MODES[0]
SQ = [float(value * value) for value in SIG]
RATIO = [1.0, 1.0, SQ[2] / SQ[0], SQ[3] / SQ[1]]
INTO = SIG[:, None] * MODES.T
MID = [float(MODES[1, mode] / SIG[mode]) for mode in range(4)]
REST = SIG[:, None] * TRANSFER.T / SIG[None, :]
EXT = SIG[:, None] * TRANSFER / SIG[None, :]


def level_scales(level):
    size_x = 2.0**level
    size_y = 2.0 ** min(level, LOC)
    return (size_y * size_y / size_x, size_x, size_x, size_x * size_y * size_y)


def roll(value, shift, axis):
    size = value.shape[axis]
    shift = shift % size
    if shift == 0:
        return value
    return pltpu.roll(value, shift, axis % value.ndim)


def iota(shape, axis):
    return lax.broadcasted_iota(jnp.int32, shape, axis)


def combine(row, parts):
    total = None
    for factor, part in zip(row, parts):
        term = part * float(factor)
        total = term if total is None else total + term
    return total


def into_modes(s0, s1, s2, s3):
    e0, e1, o0, o1 = (s0 + s3, s1 + s2, s0 - s3, s1 - s2)
    return [
        combine((INTO[mode, 0], INTO[mode, 1]), (e0, e1) if PAR[mode] > 0 else (o0, o1))
        for mode in range(4)
    ]


def from_modes(x0, x1, x2, x3):
    even, odd = (x0 + x2, x1 + x3)
    inner_even = x0 * MID[0] + x2 * MID[2]
    inner_odd = x1 * MID[1] + x3 * MID[3]
    return [even + odd, inner_even + inner_odd, inner_even - inner_odd, even - odd]


def restrict4(first, second):
    plus = [a + b for a, b in zip(first, second)]
    minus = [a - b for a, b in zip(first, second)]
    even = (plus[0], minus[1], plus[2], minus[3])
    odd = (minus[0], plus[1], minus[2], plus[3])
    return [combine(REST[mode], even if PAR[mode] > 0 else odd) for mode in range(4)]


def extend4(parts, sign):
    x0, x1, x2, x3 = parts
    out = []
    for mode in range(4):
        same, other = ((x0, x2), (x1, x3))
        row_same, row_other = ((EXT[mode, 0], EXT[mode, 2]), (EXT[mode, 1], EXT[mode, 3]))
        if PAR[mode] < 0:
            same, other, row_same, row_other = (other, same, row_other, row_same)
        out.append(combine(row_same, same) + sign * combine(row_other, other))
    return out


def extend4_mirrored(parts, sign):
    x0, x1, x2, x3 = parts
    one, two = ([], [])
    for mode in range(4):
        same, other = ((x0, x2), (x1, x3))
        row_same, row_other = ((EXT[mode, 0], EXT[mode, 2]), (EXT[mode, 1], EXT[mode, 3]))
        if PAR[mode] < 0:
            same, other, row_same, row_other = (other, same, row_other, row_same)
        a, b = (combine(row_same, same), sign * combine(row_other, other))
        one.append(a + b)
        two.append(a - b)
    return one, two


def extend4_pair(parts):
    x0, x1, x2, x3 = parts
    low, high = ([], [])
    for mode in range(4):
        same, other = ((x0, x2), (x1, x3))
        row_same, row_other = ((EXT[mode, 0], EXT[mode, 2]), (EXT[mode, 1], EXT[mode, 3]))
        if PAR[mode] < 0:
            same, other, row_same, row_other = (other, same, row_other, row_same)
        a, b = (combine(row_same, same), combine(row_other, other))
        low.append(a + b)
        high.append(a - b)
    return low, high


def inverse_tables(g_ref, d_ref, coefficient, level):
    wide_x, wide_y, wide_z, volume = level_scales(level)
    done = {}
    for i in range(4):
        for j in range(4):
            for k in range(4):
                key = (i,) + tuple(sorted((j, k)))
                if wide_x == wide_y:
                    key = tuple(sorted((i, j, k)))
                if key not in done:
                    spectrum = float(wide_x * LAM[i] + wide_y * LAM[j] + wide_z * LAM[k])
                    diagonal = coefficient * spectrum + SHIFT * volume
                    done[key] = (OMEGA / diagonal, diagonal)
                g_ref[i, j, k] = done[key][0]
                d_ref[i, j, k] = done[key][1]


def first_guess(x_ref, b_ref, g_ref):
    for i in range(4):
        for j in range(4):
            x_ref[i, j] = g_ref[i, j] * b_ref[i, j]


def face_pair(x_ref, axis, line):
    if axis == 0:
        parts = [x_ref[mode, line] for mode in range(4)]
    elif axis == 1:
        parts = [x_ref[line, mode] for mode in range(4)]
    else:
        parts = [x_ref[line, :, mode] for mode in range(4)]
    even, odd = (parts[0] + parts[2], parts[1] + parts[3])
    return even + odd, even - odd


def weigh(value, mode):
    return value if mode < 2 else value * RATIO[mode]


def neighbours(f_ref, i, j):
    along_z = [weigh(f_ref[2, k % 2, i, j], k) for k in range(4)]
    return weigh(f_ref[1, j % 2, i], j) + jnp.stack(along_z, axis=0)


def flux_yz(b_ref, f_ref, i, j):
    return b_ref[i, j] + neighbours(f_ref, i, j)


def face_pair2(x_ref, axis, first, second):
    if axis == 0:
        parts = [x_ref[mode, first, second] for mode in range(4)]
    elif axis == 1:
        parts = [x_ref[first, mode, second] for mode in range(4)]
    else:
        parts = [x_ref[first, second, mode] for mode in range(4)]
    even, odd = (parts[0] + parts[2], parts[1] + parts[3])
    return even + odd, even - odd


def flux_at(f_ref, i, j, k):
    add = weigh(f_ref[0, i % 2, j, k], i) + weigh(f_ref[1, j % 2, i, k], j)
    return add + weigh(f_ref[2, k % 2, i, j], k)


def sweep(x_ref, b_ref, g_ref, f_ref):
    for i in range(4):
        for j in range(4):
            for k in range(4):
                add = b_ref[i, j, k] + flux_at(f_ref, i, j, k)
                x_ref[i, j, k] = x_ref[i, j, k] * KEEP + g_ref[i, j, k] * add


def residual(r_ref, x_ref, b_ref, d_ref, f_ref):
    for i in range(4):
        for j in range(4):
            for k in range(4):
                add = b_ref[i, j, k] + flux_at(f_ref, i, j, k)
                r_ref[i, j, k] = add - d_ref[i, j, k] * x_ref[i, j, k]


class Halo:
    def __init__(self, rows, stride, x, b, g, d, r, t, f, coefficient, wide, orientation, signs):
        self.rows, self.stride = (rows, stride)
        self.x, self.b, self.g, self.d, self.r, self.t, self.f = (x, b, g, d, r, t, f)
        self.coefficient, self.wide = (coefficient, wide)
        self.orientation, self.signs = (orientation, signs)

    def send(self, link):
        rows, stride = (self.rows, self.stride)
        low_rows = iota((4, 8, 128), 1) < 4
        lane = iota((rows, 128), 1)
        firsts, lasts = ([], [])
        for j in range(4):
            low, high = face_pair(self.x, 0, j)
            up, down = (roll(high, 4, 1), roll(low, rows - 4, 1))
            self.t[0, 0, j] = up
            self.t[0, 1, j] = down
            firsts.append((up[:, :8], low[:, :8]))
            lasts.append((high[:, rows - 8 :], down[:, rows - 8 :]))
        for j in range(2):
            link.px[0, j] = jnp.where(low_rows, firsts[j][0], lasts[j + 2][0])
            link.px[1, j] = jnp.where(low_rows, firsts[j][1], lasts[j + 2][1])
        link.start_x()
        packed_high = packed_low = jnp.zeros((rows, 128), F32)
        for i in range(4):
            low, high = face_pair(self.x, 2, i)
            self.t[2, 0, i] = roll(high, stride, 2)
            self.t[2, 1, i] = roll(low, 128 - stride, 2)
            for j in range(4):
                spot = 4 * i + j
                packed_high = jnp.where(lane == spot, roll(high[j], spot + stride, 1), packed_high)
                packed_low = jnp.where(lane == spot, roll(low[j], spot, 1), packed_low)
        link.pz[0] = packed_high
        link.pz[1] = packed_low
        link.start_z()
        for i in range(4):
            low, high = face_pair(self.x, 1, i)
            self.t[1, 0, i] = roll(high, stride, 1)
            self.t[1, 1, i] = roll(low, rows - stride, 1)
            link.py[0, i] = high
            link.py[1, i] = low
        link.start_y()

    def merge(self, axis):
        for line, even, odd in self.merged(axis):
            self.f[axis, 0, line] = even
            self.f[axis, 1, line] = odd

    def merged(self, axis):
        rows = self.rows
        value = self.coefficient[...]
        even = (value * (TAU * self.wide * SQ[0]))[None]
        odd = (value * (TAU * self.wide * SQ[1]))[None]
        for line in range(4):
            pair = []
            for side in range(2):
                value = self.t[axis, side, line]
                if self.orientation is not None:
                    face = 2 * axis + side
                    swap = jnp.broadcast_to(self.orientation[face][None], (4, rows, 128)) % 2 == 1
                    value = jnp.where(swap, self.t[axis, side, :, line], value)
                    value = value * self.signs[face, line % 2]
                pair.append(value)
            yield line, even * (pair[0] + pair[1]), odd * (pair[0] - pair[1])

    def land_y(self, link):
        rows, stride = (self.rows, self.stride)
        link.wait_y()
        inner = iota((4, rows, 128), 1) % 4
        back = 4 - stride
        for i in range(4):
            self.t[1, 0, i] = jnp.where(inner == 0, roll(link.qy[0, i], rows - back, 1), self.t[1, 0, i])
            self.t[1, 1, i] = jnp.where(inner == back, roll(link.qy[1, i], back, 1), self.t[1, 1, i])

    def land_z(self, link):
        rows, stride = (self.rows, self.stride)
        link.wait_z()
        lane = iota((rows, 128), 1)
        high, low = (link.qz[0], link.qz[1])
        for i in range(4):
            for j in range(4):
                spot = 4 * i + j
                self.t[2, 0, i, j] = jnp.where(lane == 0, roll(high, 128 - spot, 1), self.t[2, 0, i, j])
                self.t[2, 1, i, j] = jnp.where(
                    lane == 128 - stride, roll(low, 128 - stride - spot, 1), self.t[2, 1, i, j]
                )

    def land_x(self, link):
        rows = self.rows
        link.wait_x()
        low_rows = iota((4, 8, 128), 1) < 4
        for j in range(4):
            high, low = (link.qx[0, j % 2], link.qx[1, j % 2])
            if j < 2:
                low = roll(low, 4, 1)
            else:
                high = roll(high, 4, 1)
            self.t[0, 0, j, :, :8] = jnp.where(low_rows, high, self.t[0, 0, j, :, :8])
            self.t[0, 1, j, :, rows - 8 :] = jnp.where(low_rows, self.t[0, 1, j, :, rows - 8 :], low)

    def receive(self, link, defect, between=None):
        self.land_y(link)
        self.merge(1)
        self.land_z(link)
        self.merge(2)
        for i in range(4):
            for j in range(4):
                add = flux_yz(self.b, self.f, i, j)
                if defect:
                    self.r[i, j] = add - self.d[i, j] * self.x[i, j]
                else:
                    self.x[i, j] = self.x[i, j] * KEEP + self.g[i, j] * add
        if between is not None:
            between()
        self.land_x(link)
        for j, even, odd in self.merged(0):
            for i in range(4):
                add = weigh(even if i % 2 == 0 else odd, i)
                if defect:
                    self.r[i, j] += add
                else:
                    self.x[i, j] += self.g[i, j] * add

    def correct(self, change, halo):
        rows, stride = (self.rows, self.stride)
        row, lane = (iota((4, rows, 128), 1), iota((4, rows, 128), 2))
        low_rows = iota((4, 8, 128), 1) < 4
        for line in range(4):
            low, high = face_pair(change, 0, line)
            up, down = (roll(high, 4, 1), roll(low, rows - 4, 1))
            beyond = halo[0, line, :, :8]
            self.t[0, 0, line] = up
            self.t[0, 1, line] = down
            self.t[0, 0, line, :, :8] = jnp.where(low_rows, beyond, up[:, :8])
            self.t[0, 1, line, :, rows - 8 :] = jnp.where(low_rows, down[:, rows - 8 :], beyond)
            low, high = face_pair(change, 1, line)
            beyond = halo[1, line]
            self.t[1, 0, line] = jnp.where(row % 4 == 0, beyond, roll(high, stride, 1))
            self.t[1, 1, line] = jnp.where(row % 4 == 4 - stride, beyond, roll(low, rows - stride, 1))
            low, high = face_pair(change, 2, line)
            beyond = halo[2, line]
            self.t[2, 0, line] = jnp.where(lane == 0, beyond, roll(high, stride, 2))
            self.t[2, 1, line] = jnp.where(lane == 128 - stride, beyond, roll(low, 128 - stride, 2))
        for axis in range(3):
            self.merge(axis)
        for i in range(4):
            for j in range(4):
                add = neighbours(self.f, i, j) + weigh(self.f[0, i % 2, j], i)
                self.x[i, j] += change[i, j] * KEEP + self.g[i, j] * add


class Link:
    def __init__(self, px, qx, py, qy, pz, qz, send, recv, at):
        self.px, self.qx, self.py, self.qy, self.pz, self.qz = (px, qx, py, qy, pz, qz)
        gx, gy, gz = at

        def copy(src, dst, spot, device):
            return pltpu.make_async_remote_copy(
                src_ref=src,
                dst_ref=dst,
                send_sem=send.at[spot],
                recv_sem=recv.at[spot],
                device_id=device,
                device_id_type=MESH,
            )

        self.x_copies = [
            copy(px.at[0], qx.at[0], 0, {"gx": lax.rem(gx + 1, 32)}),
            copy(px.at[1], qx.at[1], 1, {"gx": lax.rem(gx + 31, 32)}),
        ]
        self.z_copies = [
            copy(pz.at[0], qz.at[0], 2, {"gz": lax.rem(gz + 1, 4)}),
            copy(pz.at[1], qz.at[1], 3, {"gz": lax.rem(gz + 3, 4)}),
        ]
        self.y_copies = [copy(py, qy, 4, {"gy": 1 - gy})]

    def start_x(self):
        for item in self.x_copies:
            item.start()

    def start_y(self):
        for item in self.y_copies:
            item.start()

    def start_z(self):
        for item in self.z_copies:
            item.start()

    def wait_x(self):
        for item in self.x_copies:
            item.wait_recv()

    def wait_y(self):
        for item in self.y_copies:
            item.wait_recv()

    def wait_z(self):
        for item in self.z_copies:
            item.wait_recv()

    def close(self):
        for item in self.x_copies + self.y_copies + self.z_copies:
            item.wait_send()


class Whole:
    def __init__(self, level, count, x, b, g, d, r, f, coefficient):
        self.level, self.count = (level, count)
        self.x, self.b, self.g, self.d, self.r, self.f = (x, b, g, d, r, f)
        self.coefficient = coefficient

    def faces(self):
        count = self.count
        ends = iota((count, 8, 128), 2) % 64
        value = self.coefficient[...]
        factors = [
            (value * (TAU * wide * SQ[0]), value * (TAU * wide * SQ[1]))
            for wide in level_scales(self.level)[:3]
        ]
        for first in range(4):
            for second in range(4):
                low, high = face_pair2(self.x, 0, first, second)
                before, after = (roll(high[count - 1 :], 1, 1), roll(low[:1], 7, 1))
                if count > 1:
                    before = jnp.concatenate([before, high[: count - 1]], axis=0)
                    after = jnp.concatenate([low[1:], after], axis=0)
                even, odd = factors[0]
                self.f[0, 0, first, second] = even * (before + after)
                self.f[0, 1, first, second] = odd * (before - after)
                low, high = face_pair2(self.x, 1, first, second)
                even, odd = factors[1]
                self.f[1, 0, first, second] = even * roll(high + low, 64, 2)
                self.f[1, 1, first, second] = odd * roll(high - low, 64, 2)
                low, high = face_pair2(self.x, 2, first, second)
                even, odd = factors[2]
                before = jnp.where(ends < 4, roll(high, 69, 2), roll(high, 4, 2))
                after = jnp.where(ends >= 60, roll(low, 59, 2), roll(low, 124, 2))
                self.f[2, 0, first, second] = even * (before + after)
                self.f[2, 1, first, second] = odd * (before - after)

    def tables(self):
        inverse_tables(self.g, self.d, self.coefficient[...], self.level)

    def before(self):
        first_guess(self.x, self.b, self.g)
        self.faces()
        sweep(self.x, self.b, self.g, self.f)

    def down(self, coarse):
        self.faces()
        residual(self.r, self.x, self.b, self.d, self.f)
        for j in range(4):
            for block in range(coarse.count):
                first = [self.r[i, j, :, 2 * block] for i in range(4)]
                second = [self.r[i, j, :, 2 * block + 1] for i in range(4)]
                for i, value in enumerate(restrict4(first, second)):
                    coarse.b[i, j, :, block] = value

    def up(self, coarse):
        for j in range(4):
            for block in range(coarse.count):
                low, high = extend4_pair([coarse.x[i, j, :, block] for i in range(4)])
                for i in range(4):
                    self.x[i, j, :, 2 * block] += low[i]
                    self.x[i, j, :, 2 * block + 1] += high[i]
        for step in range(2):
            self.faces()
            sweep(self.x, self.b, self.g, self.f)


class Beyond:
    def __init__(self, e, g, f, h, coefficient):
        self.e, self.g, self.f, self.h, self.coefficient = (e, g, f, h, coefficient)

    def smooth(self, count, beyond):
        value = self.coefficient[:count] * (TAU * level_scales(1)[0])
        even, odd = (value * SQ[0], value * SQ[1])
        low_rows = iota((8, 128), 0) < 4
        row, lane = (iota((count, 8, 128), 1) % 4, iota((count, 8, 128), 2))
        for first in range(4):
            for second in range(4):
                low, high = face_pair2(self.e, 0, first, second)
                ha, hb, hc = (high[block] for block in range(3))
                la, lb, lc = (low[block] for block in range(3))
                far = self.h[first, second] if beyond else hc
                ta, sa = (roll(ha, 4, 0), roll(la, 4, 0))
                before = [
                    jnp.where(low_rows, roll(hb, 4, 0), ta), jnp.where(low_rows, ta, hc), jnp.where(low_rows, hb, far)
                ]
                after = [
                    jnp.where(low_rows, sa, roll(lb, 4, 0)), jnp.where(low_rows, lc, sa), jnp.where(low_rows, far, lb)
                ]
                before, after = (jnp.stack(before[:count], axis=0), jnp.stack(after[:count], axis=0))
                self.f[0, 0, first, second, :count] = even * (before + after)
                self.f[0, 1, first, second, :count] = odd * (before - after)
                low, high = face_pair2(self.e, 1, first, second)
                low, high = (low[:count], high[:count])
                before = jnp.where(row == 0, roll(high, 5, 1), roll(high, 1, 1))
                after = jnp.where(row == 3, roll(low, 3, 1), roll(low, 7, 1))
                self.f[1, 0, first, second, :count] = even * (before + after)
                self.f[1, 1, first, second, :count] = odd * (before - after)
                low, high = face_pair2(self.e, 2, first, second)
                low, high = (low[:count], high[:count])
                before = jnp.where(
                    lane == 0, roll(high, 1, 2), jnp.where(lane == 1, roll(high, 3, 2), roll(high, 2, 2))
                )
                after = jnp.where(
                    lane == 126, roll(low, 125, 2), jnp.where(lane == 127, roll(low, 127, 2), roll(low, 126, 2))
                )
                self.f[2, 0, first, second, :count] = even * (before + after)
                self.f[2, 1, first, second, :count] = odd * (before - after)
        for i in range(4):
            for j in range(4):
                for k in range(4):
                    add = weigh(self.f[0, i % 2, j, k, :count], i) + weigh(self.f[1, j % 2, i, k, :count], j)
                    add = add + weigh(self.f[2, k % 2, i, j, :count], k)
                    self.e[i, j, k, :count] = self.e[i, j, k, :count] * KEEP + self.g[i, j, k, :count] * add


def kernel(
    source_in,
    coefficient_in,
    orientation_in,
    out,
    source, coefficient, orientation, input_sem,
    x0, b0, g0, d0, r0, t0, f0, signs,
    x1, b1, g1, d1, r1, t1, f1, c1, w1, v1,
    x2, b2, g2, d2, r2, f2, c2,
    x3, b3, g3, d3, r3, f3, c3,
    x4, b4, g4, d4, r4, f4, c4,
    px, qx, py0, qy0, pz0, qz0, py1, qy1, pz1, qz1,
    cs, call, cline, cplane, cown, cin,
    ms, mall, my, mz,
    face_send, face_recv,
    c_send, c_recv, c_send2, c_recv2,
    m_send, m_recv, m_send2, m_recv2,
    told,
    e1, ge, fe, he, ce, de, halo1, halo0, wb,
    near_y, near_z, near_x, near_send, near_recv, spare,
):
    inputs = [
        pltpu.make_async_copy(src, dst, input_sem.at[spot])
        for spot, (src, dst) in enumerate(
            ((coefficient_in, coefficient), (source_in, source), (orientation_in, orientation))
        )
    ]
    for item in inputs:
        item.start()
    gx, gy, gz = (lax.axis_index("gx"), lax.axis_index("gy"), lax.axis_index("gz"))
    slow, fast = (gx // 4, lax.rem(gx, 4))
    slow_at = pl.multiple_of(slow * 16, 16)
    slow_at8 = pl.multiple_of(slow * 8, 8)
    nearest = (0, 1, 7, 2, 6, 3, 5, 4)
    offsets = [(a, b) for a in nearest for b in range(4) if (a, b) != (0, 0)]

    def along_x(a, b):
        return {"gx": lax.rem(slow + a, 8) * 4 + lax.rem(fast + b, 4)}

    def beside(step):
        return {"gx": lax.rem(gx + step + 32, 32)}

    up_z, down_z = (lax.rem(gz + 1, 4), lax.rem(gz + 3, 4))
    around = [
        {"gy": 1 - gy},
        {"gz": up_z},
        {"gy": 1 - gy, "gz": up_z},
        {"gz": down_z},
        {"gy": 1 - gy, "gz": down_z},
    ]

    barrier = pltpu.get_barrier_semaphore()
    for device in (beside(1), beside(-1), {"gy": 1 - gy}, {"gz": up_z}, {"gz": down_z}):
        pl.semaphore_signal(barrier, inc=1, device_id=device, device_id_type=MESH)

    for item in inputs:
        item.wait()
    for i in range(4):
        for k, value in enumerate(into_modes(*[source[i, :, k] for k in range(4)])):
            b0[i, :, k] = value
    for i in range(4):
        for j, value in enumerate(into_modes(*[b0[i, j] for j in range(4)])):
            b0[i, j] = value
    for j in range(4):
        for i, value in enumerate(into_modes(*[b0[i, j] for i in range(4)])):
            b0[i, j] = value
    inverse_tables(g0, d0, coefficient[...], 0)
    first_guess(x0, b0, g0)
    for face in range(6):
        code = orientation[face]
        one = jnp.ones((16, 128), F32)
        first = jnp.where(code // 2 % 2 == 1, -one, one)
        second = jnp.where(code // 4 == 1, -one, one)
        signs[face, 0] = jnp.stack([one, second, one, second], axis=0)
        signs[face, 1] = jnp.stack([first, first * second, first, first * second], axis=0)

    row8 = iota((8, 128), 0)
    lane8 = iota((8, 128), 1)
    top, bottom = (coefficient[:8], coefficient[8:])
    value = 0.5 * (
        jnp.where(row8 < 4, top, roll(bottom, 4, 0)) + jnp.where(row8 < 4, roll(top, 4, 0), bottom)
    )
    value = 0.5 * (value + roll(value, 7, 0))
    value = 0.5 * (value + roll(value, 127, 1))
    c1[...] = value
    inverse_tables(g1, d1, value, 1)
    value = 0.5 * (value + roll(value, 4, 0))
    value = 0.5 * (value + roll(value, 6, 0))
    cs[...] = 0.5 * (value + roll(value, 126, 1))

    pl.semaphore_wait(barrier, 5)

    def tell(step):
        devices = [beside(2**step), beside(-(2**step))]
        if step == 0:
            devices.append({"gy": 1 - gy})
        for device in devices:
            pl.semaphore_signal(told.at[step], inc=1, device_id=device, device_id_type=MESH)

    def heard(step):
        pl.semaphore_wait(told.at[step], 3 if step == 0 else 2)
        if step < 3:
            tell(step + 1)

    tell(0)

    def link(level, step):
        spot = 4 * level + step
        py, qy, pz, qz = (py0, qy0, pz0, qz0) if level == 0 else (py1, qy1, pz1, qz1)
        return Link(
            px.at[spot], qx.at[spot], py.at[step], qy.at[step], pz.at[step], qz.at[step],
            face_send.at[spot], face_recv.at[spot], (gx, gy, gz),
        )

    def copy(src, dst, send, recv, device):
        return pltpu.make_async_remote_copy(
            src_ref=src, dst_ref=dst, send_sem=send, recv_sem=recv, device_id=device, device_id_type=MESH
        )

    fine = Halo(16, 1, x0, b0, g0, d0, r0, t0, f0, coefficient, 1.0, orientation, signs)
    mid = Halo(8, 2, x1, b1, g1, d1, r1, t1, f1, c1, 2.0, None, None)
    links = []

    c_line = [copy(cs, call.at[fast], c_send.at[0, b], c_recv.at[0, b], along_x(0, b)) for b in range(1, 4)]
    c_copies = [
        copy(cline, cplane.at[pl.ds(slow_at8, 8)], c_send.at[a, 0], c_recv.at[a, 0], along_x(a, 0))
        for a in nearest[1:]
    ]

    def send_line():
        for item in c_line:
            item.start()

    near_copies = [copy(c1, near_y, near_send.at[0], near_recv.at[0], {"gy": 1 - gy})]
    near_copies[0].start()
    ring = iota((8, 128), 0) % 4

    def near_step(step):
        if step == 0:
            near_copies[0].wait_recv()
            own, other = (c1[...], near_y[...])
            value = jnp.where(ring < 2, jnp.where(ring == 0, own, roll(own, 7, 0)),
                              jnp.where(ring == 2, roll(other, 2, 0), roll(other, 1, 0)))
            spare[0] = value
            for spot, device in ((1, {"gz": down_z}), (2, {"gz": up_z})):
                item = copy(spare.at[0], near_z.at[spot - 1], near_send.at[spot], near_recv.at[spot], device)
                item.start()
                near_copies.append(item)
        elif step == 1:
            near_copies[1].wait_recv()
            near_copies[2].wait_recv()
            outer = jnp.where(lane8 < 64, roll(near_z[0], 1, 1), roll(near_z[1], 1, 1))
            value = jnp.where(lane8 % 2 == 0, spare[0], outer)
            spare[1] = value
            ce[0] = value
            for spot, device in ((3, beside(-1)), (4, beside(1))):
                item = copy(spare.at[1], near_x.at[spot - 3], near_send.at[spot], near_recv.at[spot], device)
                item.start()
                near_copies.append(item)
        else:
            near_copies[3].wait_recv()
            near_copies[4].wait_recv()
            after, before = (near_x[0], near_x[1])
            ce[1] = jnp.where(row8 < 4, after, before)
            ce[2] = jnp.where(row8 < 4, roll(after, 4, 0), roll(before, 4, 0))
            inverse_tables(ge, de, ce[...], 1)

    links.append(link(0, 0))
    fine.send(links[-1])
    fine.receive(links[-1], False, lambda: (heard(0), near_step(0)))
    links.append(link(0, 1))
    fine.send(links[-1])
    fine.receive(links[-1], True, lambda: (heard(1), near_step(1), send_line()))
    row4 = iota((4, 8, 128), 1)
    lane4 = iota((4, 8, 128), 2)
    for j in range(4):
        first, second = ([], [])
        for i in range(4):
            top, bottom = (r0[i, j, :, :8], r0[i, j, :, 8:])
            first.append(jnp.where(row4 < 4, top, roll(bottom, 4, 1)))
            second.append(jnp.where(row4 < 4, roll(top, 4, 1), bottom))
        for i, value in enumerate(restrict4(first, second)):
            w1[i, j] = value
    for i in range(4):
        first = [w1[i, j] for j in range(4)]
        for j, value in enumerate(restrict4(first, [roll(item, 7, 1) for item in first])):
            v1[i, j] = value
    for i in range(4):
        first = [v1[i, :, k] for k in range(4)]
        for k, value in enumerate(restrict4(first, [roll(item, 127, 2) for item in first])):
            b1[i, :, k] = value

    first_guess(x1, b1, g1)
    links.append(link(1, 0))
    mid.send(links[-1])
    mid.receive(links[-1], False, lambda: (heard(2), near_step(2)))
    links.append(link(1, 1))
    mid.send(links[-1])
    def send_coefficients():
        heard(3)
        for item in c_line:
            item.wait_recv()
        call[fast] = cs[...]
        lines = [jnp.broadcast_to(call[block, pl.ds(0, 1), :], (8, 128)) for block in range(4)]
        cline[...] = jnp.where(row8 < 2, jnp.where(row8 == 0, lines[0], lines[1]),
                               jnp.where(row8 == 2, lines[2], lines[3]))
        for item in c_copies:
            item.start()
        cplane[pl.ds(slow_at8, 8), :] = cline[...]

    mid.receive(links[-1], True, send_coefficients)
    for j in range(4):
        first = [r1[i, j] for i in range(4)]
        for i, value in enumerate(restrict4(first, [roll(item, 4, 1) for item in first])):
            w1[i, j] = value
    for i in range(4):
        first = [w1[i, j] for j in range(4)]
        for j, value in enumerate(restrict4(first, [roll(item, 6, 1) for item in first])):
            v1[i, j] = value
    packed = []
    for i in range(4):
        first = [v1[i, :, k] for k in range(4)]
        total = None
        for k, value in enumerate(restrict4(first, [roll(item, 126, 2) for item in first])):
            total = value if k == 0 else jnp.where(lane4 % 4 == k, roll(value, k, 2), total)
        packed += [total[j] for j in range(4)]
    for line in range(8):
        low, high = (packed[line], packed[line + 8])
        ms[pl.ds(line, 1), :] = jnp.where(lane8 < 64, low, roll(high, 64, 1))[:1]
        ms[pl.ds(line + 8, 1), :] = jnp.where(lane8 < 64, roll(low, 64, 1), high)[:1]

    m_copies = {
        (a, b): copy(ms, mall.at[fast, pl.ds(slow_at, 16)], m_send.at[a, b], m_recv.at[a, b], along_x(a, b))
        for a, b in offsets
    }
    for item in m_copies.values():
        item.start()
    mall[fast, pl.ds(slow_at, 16), :] = ms[...]
    for item in c_copies:
        item.wait_recv()
    for block in range(4):
        cown[block] = cplane[pl.ds(block, 8, stride=8), :]
    c_around = [
        copy(cown, cin.at[spot], c_send2.at[spot], c_recv2.at[spot], device)
        for spot, device in enumerate(around)
    ]
    for item in c_around:
        item.start()
    for i in range(4):
        for j in range(4):
            x1[i, j] += g1[i, j] * r1[i, j]
    links.append(link(1, 2))
    mid.send(links[-1])
    passed = []
    for a in nearest:
        for b in range(4):
            if (a, b) != (0, 0):
                m_copies[a, b].wait_recv()
        start = lax.rem(slow + 8 - a, 8)
        start16 = pl.multiple_of(start * 16, 16)
        start8 = pl.multiple_of(start * 8, 8)
        upper = pl.multiple_of(start * 16 + 8, 8)
        for spot, device in enumerate(around):
            if spot == 0:
                src, dst = (mall.at[:, pl.ds(start16, 16)], my.at[:, pl.ds(start16, 16)])
            else:
                src = mall.at[:, pl.ds(upper if spot < 3 else start16, 8)]
                dst = mz.at[spot - 1, :, pl.ds(start8, 8)]
            item = copy(src, dst, m_send2.at[spot, a], m_recv2.at[spot, a], device)
            item.start()
            passed.append(item)
    for item in c_around:
        item.wait_recv()
    for block in range(4):
        mine, other = (cown[block], cin[0, block])
        below, below_other, above, above_other = (cin[spot, block] for spot in range(1, 5))
        phase = lane8 % 4
        near = jnp.where(phase == 0, roll(below, 64, 1), roll(mine, 1, 1))
        near = jnp.where(phase == 2, roll(mine, 66, 1), near)
        near = jnp.where(phase == 3, roll(above, 3, 1), near)
        far = jnp.where(phase == 0, below_other, roll(other, 65, 1))
        far = jnp.where(phase == 2, roll(other, 2, 1), far)
        far = jnp.where(phase == 3, roll(above_other, 67, 1), far)
        c2[block] = jnp.where(lane8 < 64, near, far)
    for block in range(2):
        c3[block] = 0.5 * (c2[2 * block] + c2[2 * block + 1])
    c4[0] = 0.5 * (c3[0] + c3[1])
    level2 = Whole(2, 4, x2, b2, g2, d2, r2, f2, c2)
    level3 = Whole(3, 2, x3, b3, g3, d3, r3, f3, c3)
    level4 = Whole(4, 1, x4, b4, g4, d4, r4, f4, c4)
    for level in (level2, level3, level4):
        level.tables()
    mid.receive(links[-1], False)
    links.append(link(1, 3))
    mid.send(links[-1])
    for i in range(4):
        for j in range(4):
            x0[i, j] += g0[i, j] * r0[i, j]
    for item in passed:
        item.wait_recv()

    def unpack(block, carry):
        odd, pair = (lane8 % 2 == 1, lane8 % 4 >= 2)
        for line in range(8):
            def rows(ref, start, stride):
                return ref[block, pl.ds(start, 8, stride=stride), :]

            near = [
                rows(mz.at[0], line, 8), rows(mall, line, 16), rows(mall, line + 8, 16), rows(mz.at[2], line, 8)
            ]
            far = [
                rows(mz.at[1], line, 8), rows(my, line, 16), rows(my, line + 8, 16), rows(mz.at[3], line, 8)
            ]
            for half in range(2):
                if half == 0:
                    part = [jnp.where(lane8 < 64, a, roll(b, 64, 1)) for a, b in zip(near, far)]
                else:
                    part = [jnp.where(lane8 < 64, roll(a, 64, 1), b) for a, b in zip(near, far)]
                step = [
                    jnp.where(odd, roll(part[1], 1, 1), part[0]),
                    jnp.where(odd, part[1], roll(part[0], 127, 1)),
                    jnp.where(odd, roll(part[3], 1, 1), part[2]),
                    jnp.where(odd, part[3], roll(part[2], 127, 1)),
                ]
                last = [
                    jnp.where(pair, roll(step[2], 2, 1), step[0]),
                    jnp.where(pair, roll(step[3], 2, 1), step[1]),
                    jnp.where(pair, step[2], roll(step[0], 126, 1)),
                    jnp.where(pair, step[3], roll(step[1], 126, 1)),
                ]
                mode = line + 8 * half
                for k in range(4):
                    b2[mode // 4, mode % 4, k, block] = last[k]
        return carry

    lax.fori_loop(0, 4, unpack, 0)
    level2.before()
    level2.down(level3)
    level3.before()
    level3.down(level4)
    level4.before()
    level3.up(level4)
    level2.up(level3)

    def element(step):
        place = lax.rem(gx + step + 32, 32)
        return place // 4, lax.rem(place, 4)

    def take(i, j, step):
        at, block = element(step)
        return jnp.broadcast_to(x2[i, j, :, block, pl.ds(at, 1), :], (4, 8, 128))

    def spread(value):
        value = jnp.where(row4 % 4 < 2, value, roll(value, 64, 2))
        low = jnp.where(lane4 % 2 == 0, roll(value, 127, 2), roll(value, 126, 2))
        high = jnp.where(lane4 % 2 == 0, roll(value, 62, 2), roll(value, 65, 2))
        value = jnp.where(lane4 < 64, low, high)
        return jnp.where(lane4 % 4 < 2, value, roll(value, 2, 2))

    one = jnp.ones((4, 8, 128), F32)
    sign_z = jnp.where(lane4 % 4 < 2, one, -one)
    sign_y = jnp.where(row4 % 2 == 0, one, -one)
    sign_x = jnp.where(row4 < 4, one, -one)
    for i in range(4):
        for j in range(4):
            w1[i, j] = spread(take(i, j, 0))
            wb[i, j] = spread(jnp.where(row4 < 4, take(i, j, 1), take(i, j, -1)))
    for j in range(4):
        after = [take(i, j, 2) for i in range(4)]
        before = [take(i, j, -2) for i in range(4)]
        low = (after[0] + after[2]) + (after[1] + after[3])
        high = (before[0] + before[2]) - (before[1] + before[3])
        he[j] = spread(jnp.where(row4 < 4, low, high))
    for ref in (w1, wb):
        for i in range(4):
            for k, value in enumerate(extend4([ref[i, :, k] for k in range(4)], sign_z)):
                ref[i, :, k] = value
        for i in range(4):
            for j, value in enumerate(extend4([ref[i, j] for j in range(4)], sign_y)):
                ref[i, j] = value
    for k, value in enumerate(extend4([he[:, k] for k in range(4)], sign_z)):
        he[:, k] = value
    for j, value in enumerate(extend4([he[j] for j in range(4)], sign_y)):
        he[j] = value
    for j in range(4):
        for i, value in enumerate(extend4([w1[i, j] for i in range(4)], sign_x)):
            e1[i, j, :, 0] = value
        for i, (value, other) in enumerate(zip(*extend4_mirrored([wb[i, j] for i in range(4)], sign_x))):
            e1[i, j, :, 1] = value
            e1[i, j, :, 2] = other
    beyond = Beyond(e1, ge, fe, he, ce)
    beyond.smooth(3, True)
    beyond.smooth(2, False)

    mid.land_y(links[-1])
    mid.land_z(links[-1])
    mid.land_x(links[-1])

    def own_rows(value):
        return jnp.where(row4 % 4 == 2, roll(value, 1, 1), value)

    for line in range(4):
        parts = [e1[i, line, :, 1] for i in range(4)]
        even, odd = (parts[0] + parts[2], parts[1] + parts[3])
        value = own_rows(roll(jnp.where(row4 < 4, even + odd, even - odd), 4, 1))
        halo1[0, line] = value + jnp.where(row4 < 4, t1[0, 0, line], t1[0, 1, line])
        parts = [e1[line, j, :, 0] for j in range(4)]
        even, odd = (parts[0] + parts[2], parts[1] + parts[3])
        value = jnp.where(row4 % 4 == 0, roll(even - odd, 5, 1), even + odd)
        halo1[1, line] = value + jnp.where(row4 % 4 == 0, t1[1, 0, line], t1[1, 1, line])
        parts = [e1[line, :, k, 0] for k in range(4)]
        even, odd = (parts[0] + parts[2], parts[1] + parts[3])
        value = own_rows(jnp.where(lane4 < 64, roll(even - odd, 1, 2), roll(even + odd, 125, 2)))
        halo1[2, line] = value + jnp.where(lane4 < 64, t1[2, 0, line], t1[2, 1, line])

    def fill(value):
        value = jnp.where(row4 % 2 == 0, value, roll(value, 1, 1))
        return jnp.where(lane4 % 2 == 0, value, roll(value, 1, 2))

    def doubled(value):
        turned = roll(value, 4, 1)
        low, high = (jnp.where(row4 < 4, value, turned), jnp.where(row4 < 4, turned, value))
        return jnp.concatenate([low, high], axis=1)

    for i in range(4):
        for j in range(4):
            w1[i, j] = fill(x1[i, j] + own_rows(e1[i, j, :, 0]))
    for axis in range(3):
        for line in range(4):
            halo1[axis, line] = fill(halo1[axis, line])
    sign_z = jnp.where(lane4 % 2 == 0, one, -one)
    wide_one = jnp.ones((4, 16, 128), F32)
    sign_x = jnp.where(iota((4, 16, 128), 1) % 8 < 4, wide_one, -wide_one)
    for i in range(4):
        for k, value in enumerate(extend4([w1[i, :, k] for k in range(4)], sign_z)):
            w1[i, :, k] = value
    for i in range(4):
        for j, value in enumerate(extend4([w1[i, j] for j in range(4)], sign_y)):
            w1[i, j] = value
    for j in range(4):
        for i, value in enumerate(extend4([doubled(w1[i, j]) for i in range(4)], sign_x)):
            r0[i, j] = value
    for axis in range(2):
        for k, value in enumerate(extend4([halo1[axis, :, k] for k in range(4)], sign_z)):
            halo1[axis, :, k] = value
    for line, value in enumerate(extend4([halo1[0, line] for line in range(4)], sign_y)):
        halo0[0, line, :, :8] = value
    for line, value in enumerate(extend4([doubled(halo1[1, line]) for line in range(4)], sign_x)):
        halo0[1, line] = value
    for line, value in enumerate(extend4([halo1[2, :, line] for line in range(4)], sign_y)):
        halo1[2, :, line] = value
    for line, value in enumerate(extend4([doubled(halo1[2, line]) for line in range(4)], sign_x)):
        halo0[2, line] = value
    fine.correct(r0, halo0)
    links.append(link(0, 2))
    fine.send(links[-1])
    fine.receive(links[-1], False)

    for i in range(4):
        for k, value in enumerate(from_modes(*[x0[i, :, k] for k in range(4)])):
            out[i, :, k] = value
    for i in range(4):
        for j, value in enumerate(from_modes(*[out[i, j] for j in range(4)])):
            out[i, j] = value
    for j in range(4):
        for i, value in enumerate(from_modes(*[out[i, j] for i in range(4)])):
            out[i, j] = value

    for item in links:
        item.close()
    for item in near_copies + c_line + c_copies + c_around + list(m_copies.values()) + passed:
        item.wait_send()


def scratch():
    def mem(*shape):
        return pltpu.VMEM(shape, F32)

    modes = (4, 4, 4)
    dma = pltpu.SemaphoreType.DMA
    inputs = [mem(*modes, 16, 128), mem(16, 128), pltpu.VMEM((6, 16, 128), jnp.int32), dma((3,))]
    level0 = [mem(*modes, 16, 128)] * 5 + [
        mem(3, 2, 4, 4, 16, 128), mem(3, 2, 4, 4, 16, 128), mem(6, 2, 4, 16, 128)
    ]
    level1 = [mem(*modes, 8, 128)] * 5 + [
        mem(3, 2, 4, 4, 8, 128), mem(3, 2, 4, 4, 8, 128), mem(8, 128), mem(*modes, 8, 128), mem(*modes, 8, 128)
    ]
    whole = []
    for count in (4, 2, 1):
        whole += [mem(*modes, count, 8, 128)] * 5 + [mem(3, 2, 4, 4, count, 8, 128), mem(count, 8, 128)]
    faces = [
        mem(8, 2, 2, 4, 8, 128), mem(8, 2, 2, 4, 8, 128),
        mem(4, 2, 4, 4, 16, 128), mem(4, 2, 4, 4, 16, 128), mem(4, 2, 16, 128), mem(4, 2, 16, 128),
        mem(4, 2, 4, 4, 8, 128), mem(4, 2, 4, 4, 8, 128), mem(4, 2, 8, 128), mem(4, 2, 8, 128),
    ]
    gathered = [
        mem(8, 128), mem(4, 8, 128), mem(8, 128), mem(64, 128), mem(4, 8, 128), mem(5, 4, 8, 128),
        mem(16, 128), mem(4, 128, 128), mem(4, 128, 128), mem(4, 4, 64, 128),
    ]
    sems = [dma((8, 5)), dma((8, 5)), dma((8, 4)), dma((8, 4)), dma((5,)), dma((5,)),
            dma((8, 4)), dma((8, 4)), dma((5, 8)), dma((5, 8)),
            pltpu.SemaphoreType.REGULAR((4,))]
    extended = [
        mem(*modes, 3, 8, 128), mem(*modes, 3, 8, 128), mem(3, 2, 4, 4, 3, 8, 128), mem(4, 4, 8, 128),
        mem(3, 8, 128), mem(*modes, 3, 8, 128), mem(3, 4, 4, 8, 128), mem(3, 4, 4, 16, 128), mem(*modes, 8, 128),
        mem(8, 128), mem(2, 8, 128), mem(2, 8, 128), dma((5,)), dma((5,)), mem(2, 8, 128),
    ]
    return inputs + level0 + level1 + whole + faces + gathered + sems + extended


def local(source, coefficient, orientation):
    vmem = pl.BlockSpec(memory_space=pltpu.VMEM)
    out = pl.pallas_call(
        kernel,
        out_shape=jax.ShapeDtypeStruct((4, 4, 4, 16, 128), F32),
        in_specs=[pl.BlockSpec(memory_space=pl.ANY)] * 3,
        out_specs=vmem,
        scratch_shapes=scratch(),
        compiler_params=pltpu.CompilerParams(
            collective_id=0, has_side_effects=True, vmem_limit_bytes=64 * 1024 * 1024 - 65536
        ),
    )(
        source.reshape(4, 4, 4, 16, 128),
        coefficient.reshape(16, 128),
        orientation.reshape(6, 16, 128),
    )
    return out.reshape(4, 4, 4, 4, 4, 128)


def solution(mesh):
    in_specs = (
        P(None, None, None, "gx", "gy", "gz"),
        P("gx", "gy", "gz"),
        P(None, "gx", "gy", "gz"),
    )
    out_specs = P(None, None, None, "gx", "gy", "gz")
    return jax.shard_map(local, mesh=mesh, in_specs=in_specs, out_specs=out_specs, check_vma=False)
```

```python
import math

import jax
import jax.numpy as jnp
import numpy as np
from jax import lax
from jax.experimental import pallas as pl
from jax.experimental.pallas import tpu as pltpu
from jax.sharding import PartitionSpec as P

LOC = 2
TAU = 6.0
SHIFT = 1.0
OMEGA = 0.8
KEEP = 0.2
MESH = pl.DeviceIdType.MESH
F32 = jnp.float32


def lagrange(points, node_points):
    table = np.ones((points.shape[0], 4))
    for column in range(4):
        for other in range(4):
            if other != column:
                table[:, column] *= (points - node_points[other]) / (
                    node_points[column] - node_points[other]
                )
    return table


def jacobi_eigen(matrix):
    current = matrix.copy()
    vectors = np.eye(4)
    for sweep in range(12):
        for first in range(3):
            for second in range(first + 1, 4):
                angle = 0.5 * math.atan2(
                    2.0 * current[first, second], current[second, second] - current[first, first]
                )
                cosine = math.cos(angle)
                sine = math.sin(angle)
                rotation = np.eye(4)
                rotation[first, first] = cosine
                rotation[second, second] = cosine
                rotation[first, second] = sine
                rotation[second, first] = -sine
                current = rotation.T @ current @ rotation
                vectors = vectors @ rotation
    return (np.array([current[index, index] for index in range(4)]), vectors)


def tables():
    node_points = np.array([-1.0, -1.0 / math.sqrt(5.0), 1.0 / math.sqrt(5.0), 1.0])
    weights = np.array([1.0, 5.0, 5.0, 1.0]) / 6.0
    derivative = np.zeros((4, 4))
    for column in range(4):
        for other in range(4):
            if other != column:
                term = np.full(4, 1.0 / (node_points[column] - node_points[other]))
                for third in range(4):
                    if third != column and third != other:
                        term = (
                            term
                            * (node_points - node_points[third])
                            / (node_points[column] - node_points[third])
                        )
                derivative[:, column] += term
    stiffness = derivative.T @ (weights[:, None] * derivative)
    stiffness[0, 0] += TAU
    stiffness[3, 3] += TAU
    scale = weights ** (-0.5)
    eigen_values, eigen_vectors = jacobi_eigen(scale[:, None] * stiffness * scale[None, :])
    modes = scale[:, None] * eigen_vectors
    order = sorted(range(4), key=lambda mode: eigen_values[mode])
    eigen_values, modes = (eigen_values[order], modes[:, order])
    child = lagrange((node_points - 1.0) / 2.0, node_points)
    transfer = modes.T @ (weights[:, None] * (child @ modes))
    return (eigen_values, modes, transfer)


LAM, MODES, TRANSFER = tables()
PAR = (1.0, -1.0, 1.0, -1.0)
SIG = MODES[0]
SQ = [float(value * value) for value in SIG]
RATIO = [1.0, 1.0, SQ[2] / SQ[0], SQ[3] / SQ[1]]
INTO = SIG[:, None] * MODES.T
MID = [float(MODES[1, mode] / SIG[mode]) for mode in range(4)]
REST = SIG[:, None] * TRANSFER.T / SIG[None, :]
EXT = SIG[:, None] * TRANSFER / SIG[None, :]


def level_scales(level):
    size_x = 2.0**level
    size_y = 2.0 ** min(level, LOC)
    return (size_y * size_y / size_x, size_x, size_x, size_x * size_y * size_y)


def roll(value, shift, axis):
    size = value.shape[axis]
    shift = shift % size
    if shift == 0:
        return value
    return pltpu.roll(value, shift, axis % value.ndim)


def iota(shape, axis):
    return lax.broadcasted_iota(jnp.int32, shape, axis)


def combine(row, parts):
    total = None
    for factor, part in zip(row, parts):
        term = part * float(factor)
        total = term if total is None else total + term
    return total


def into_modes(s0, s1, s2, s3):
    e0, e1, o0, o1 = (s0 + s3, s1 + s2, s0 - s3, s1 - s2)
    return [
        combine((INTO[mode, 0], INTO[mode, 1]), (e0, e1) if PAR[mode] > 0 else (o0, o1))
        for mode in range(4)
    ]


def from_modes(x0, x1, x2, x3):
    even, odd = (x0 + x2, x1 + x3)
    inner_even = x0 * MID[0] + x2 * MID[2]
    inner_odd = x1 * MID[1] + x3 * MID[3]
    return [even + odd, inner_even + inner_odd, inner_even - inner_odd, even - odd]


def restrict4(first, second):
    plus = [a + b for a, b in zip(first, second)]
    minus = [a - b for a, b in zip(first, second)]
    even = (plus[0], minus[1], plus[2], minus[3])
    odd = (minus[0], plus[1], minus[2], plus[3])
    return [combine(REST[mode], even if PAR[mode] > 0 else odd) for mode in range(4)]


def extend4(parts, sign):
    x0, x1, x2, x3 = parts
    out = []
    for mode in range(4):
        same, other = ((x0, x2), (x1, x3))
        row_same, row_other = ((EXT[mode, 0], EXT[mode, 2]), (EXT[mode, 1], EXT[mode, 3]))
        if PAR[mode] < 0:
            same, other, row_same, row_other = (other, same, row_other, row_same)
        out.append(combine(row_same, same) + sign * combine(row_other, other))
    return out


def extend4_mirrored(parts, sign):
    x0, x1, x2, x3 = parts
    one, two = ([], [])
    for mode in range(4):
        same, other = ((x0, x2), (x1, x3))
        row_same, row_other = ((EXT[mode, 0], EXT[mode, 2]), (EXT[mode, 1], EXT[mode, 3]))
        if PAR[mode] < 0:
            same, other, row_same, row_other = (other, same, row_other, row_same)
        a, b = (combine(row_same, same), sign * combine(row_other, other))
        one.append(a + b)
        two.append(a - b)
    return one, two


def extend4_pair(parts):
    x0, x1, x2, x3 = parts
    low, high = ([], [])
    for mode in range(4):
        same, other = ((x0, x2), (x1, x3))
        row_same, row_other = ((EXT[mode, 0], EXT[mode, 2]), (EXT[mode, 1], EXT[mode, 3]))
        if PAR[mode] < 0:
            same, other, row_same, row_other = (other, same, row_other, row_same)
        a, b = (combine(row_same, same), combine(row_other, other))
        low.append(a + b)
        high.append(a - b)
    return low, high


def inverse_tables(g_ref, d_ref, coefficient, level):
    wide_x, wide_y, wide_z, volume = level_scales(level)
    done = {}
    for i in range(4):
        for j in range(4):
            for k in range(4):
                key = (i,) + tuple(sorted((j, k)))
                if wide_x == wide_y:
                    key = tuple(sorted((i, j, k)))
                if key not in done:
                    spectrum = float(wide_x * LAM[i] + wide_y * LAM[j] + wide_z * LAM[k])
                    diagonal = coefficient * spectrum + SHIFT * volume
                    done[key] = (OMEGA / diagonal, diagonal)
                g_ref[i, j, k] = done[key][0]
                d_ref[i, j, k] = done[key][1]


def first_guess(x_ref, b_ref, g_ref):
    for i in range(4):
        for j in range(4):
            x_ref[i, j] = g_ref[i, j] * b_ref[i, j]


def face_pair(x_ref, axis, line):
    if axis == 0:
        parts = [x_ref[mode, line] for mode in range(4)]
    elif axis == 1:
        parts = [x_ref[line, mode] for mode in range(4)]
    else:
        parts = [x_ref[line, :, mode] for mode in range(4)]
    even, odd = (parts[0] + parts[2], parts[1] + parts[3])
    return even + odd, even - odd


def weigh(value, mode):
    return value if mode < 2 else value * RATIO[mode]


def neighbours(f_ref, i, j):
    along_z = [weigh(f_ref[2, k % 2, i, j], k) for k in range(4)]
    return weigh(f_ref[1, j % 2, i], j) + jnp.stack(along_z, axis=0)


def flux_yz(b_ref, f_ref, i, j):
    return b_ref[i, j] + neighbours(f_ref, i, j)


def face_pair2(x_ref, axis, first, second):
    if axis == 0:
        parts = [x_ref[mode, first, second] for mode in range(4)]
    elif axis == 1:
        parts = [x_ref[first, mode, second] for mode in range(4)]
    else:
        parts = [x_ref[first, second, mode] for mode in range(4)]
    even, odd = (parts[0] + parts[2], parts[1] + parts[3])
    return even + odd, even - odd


def flux_at(f_ref, i, j, k):
    add = weigh(f_ref[0, i % 2, j, k], i) + weigh(f_ref[1, j % 2, i, k], j)
    return add + weigh(f_ref[2, k % 2, i, j], k)


def sweep(x_ref, b_ref, g_ref, f_ref):
    for i in range(4):
        for j in range(4):
            for k in range(4):
                add = b_ref[i, j, k] + flux_at(f_ref, i, j, k)
                x_ref[i, j, k] = x_ref[i, j, k] * KEEP + g_ref[i, j, k] * add


def residual(r_ref, x_ref, b_ref, d_ref, f_ref):
    for i in range(4):
        for j in range(4):
            for k in range(4):
                add = b_ref[i, j, k] + flux_at(f_ref, i, j, k)
                r_ref[i, j, k] = add - d_ref[i, j, k] * x_ref[i, j, k]


class Halo:
    def __init__(self, rows, stride, x, b, g, d, r, t, f, coefficient, wide, orientation, signs):
        self.rows, self.stride = (rows, stride)
        self.x, self.b, self.g, self.d, self.r, self.t, self.f = (x, b, g, d, r, t, f)
        self.coefficient, self.wide = (coefficient, wide)
        self.orientation, self.signs = (orientation, signs)

    def send(self, link, after_x=None):
        rows, stride = (self.rows, self.stride)
        low_rows = iota((4, 8, 128), 1) < 4
        lane = iota((rows, 128), 1)
        firsts, lasts = ([], [])
        for j in range(4):
            low, high = face_pair(self.x, 0, j)
            up, down = (roll(high, 4, 1), roll(low, rows - 4, 1))
            self.t[0, 0, j] = up
            self.t[0, 1, j] = down
            firsts.append((up[:, :8], low[:, :8]))
            lasts.append((high[:, rows - 8 :], down[:, rows - 8 :]))
        for j in range(2):
            link.px[0, j] = jnp.where(low_rows, firsts[j][0], lasts[j + 2][0])
            link.px[1, j] = jnp.where(low_rows, firsts[j][1], lasts[j + 2][1])
        link.start_x()
        if after_x is not None:
            after_x()
        packed_high = packed_low = jnp.zeros((rows, 128), F32)
        for i in range(4):
            low, high = face_pair(self.x, 2, i)
            self.t[2, 0, i] = roll(high, stride, 2)
            self.t[2, 1, i] = roll(low, 128 - stride, 2)
            for j in range(4):
                spot = 4 * i + j
                packed_high = jnp.where(lane == spot, roll(high[j], spot + stride, 1), packed_high)
                packed_low = jnp.where(lane == spot, roll(low[j], spot, 1), packed_low)
        link.pz[0] = packed_high
        link.pz[1] = packed_low
        link.start_z()
        for i in range(4):
            low, high = face_pair(self.x, 1, i)
            self.t[1, 0, i] = roll(high, stride, 1)
            self.t[1, 1, i] = roll(low, rows - stride, 1)
            link.py[0, i] = high
            link.py[1, i] = low
        link.start_y()

    def merge(self, axis):
        for line, even, odd in self.merged(axis):
            self.f[axis, 0, line] = even
            self.f[axis, 1, line] = odd

    def merged(self, axis):
        rows = self.rows
        value = self.coefficient[...]
        even = (value * (TAU * self.wide * SQ[0]))[None]
        odd = (value * (TAU * self.wide * SQ[1]))[None]
        for line in range(4):
            pair = []
            for side in range(2):
                value = self.t[axis, side, line]
                if self.orientation is not None:
                    face = 2 * axis + side
                    swap = jnp.broadcast_to(self.orientation[face][None], (4, rows, 128)) % 2 == 1
                    value = jnp.where(swap, self.t[axis, side, :, line], value)
                    value = value * self.signs[face, line % 2]
                pair.append(value)
            yield line, even * (pair[0] + pair[1]), odd * (pair[0] - pair[1])

    def land_y(self, link):
        rows, stride = (self.rows, self.stride)
        link.wait_y()
        inner = iota((4, rows, 128), 1) % 4
        back = 4 - stride
        for i in range(4):
            self.t[1, 0, i] = jnp.where(inner == 0, roll(link.qy[0, i], rows - back, 1), self.t[1, 0, i])
            self.t[1, 1, i] = jnp.where(inner == back, roll(link.qy[1, i], back, 1), self.t[1, 1, i])

    def land_z(self, link):
        rows, stride = (self.rows, self.stride)
        link.wait_z()
        lane = iota((rows, 128), 1)
        high, low = (link.qz[0], link.qz[1])
        for i in range(4):
            for j in range(4):
                spot = 4 * i + j
                self.t[2, 0, i, j] = jnp.where(lane == 0, roll(high, 128 - spot, 1), self.t[2, 0, i, j])
                self.t[2, 1, i, j] = jnp.where(
                    lane == 128 - stride, roll(low, 128 - stride - spot, 1), self.t[2, 1, i, j]
                )

    def land_x(self, link):
        rows = self.rows
        link.wait_x()
        low_rows = iota((4, 8, 128), 1) < 4
        for j in range(4):
            high, low = (link.qx[0, j % 2], link.qx[1, j % 2])
            if j < 2:
                low = roll(low, 4, 1)
            else:
                high = roll(high, 4, 1)
            self.t[0, 0, j, :, :8] = jnp.where(low_rows, high, self.t[0, 0, j, :, :8])
            self.t[0, 1, j, :, rows - 8 :] = jnp.where(low_rows, self.t[0, 1, j, :, rows - 8 :], low)

    def receive(self, link, defect, between=None):
        self.land_y(link)
        self.merge(1)
        self.land_z(link)
        self.merge(2)
        for i in range(4):
            for j in range(4):
                add = flux_yz(self.b, self.f, i, j)
                if defect:
                    self.r[i, j] = add - self.d[i, j] * self.x[i, j]
                else:
                    self.x[i, j] = self.x[i, j] * KEEP + self.g[i, j] * add
        if between is not None:
            between()
        self.land_x(link)
        for j, even, odd in self.merged(0):
            for i in range(4):
                add = weigh(even if i % 2 == 0 else odd, i)
                if defect:
                    self.r[i, j] += add
                else:
                    self.x[i, j] += self.g[i, j] * add

    def correct(self, change, halo):
        rows, stride = (self.rows, self.stride)
        row, lane = (iota((4, rows, 128), 1), iota((4, rows, 128), 2))
        low_rows = iota((4, 8, 128), 1) < 4
        for line in range(4):
            low, high = face_pair(change, 0, line)
            up, down = (roll(high, 4, 1), roll(low, rows - 4, 1))
            beyond = halo[0, line, :, :8]
            self.t[0, 0, line] = up
            self.t[0, 1, line] = down
            self.t[0, 0, line, :, :8] = jnp.where(low_rows, beyond, up[:, :8])
            self.t[0, 1, line, :, rows - 8 :] = jnp.where(low_rows, down[:, rows - 8 :], beyond)
            low, high = face_pair(change, 1, line)
            beyond = halo[1, line]
            self.t[1, 0, line] = jnp.where(row % 4 == 0, beyond, roll(high, stride, 1))
            self.t[1, 1, line] = jnp.where(row % 4 == 4 - stride, beyond, roll(low, rows - stride, 1))
            low, high = face_pair(change, 2, line)
            beyond = halo[2, line]
            self.t[2, 0, line] = jnp.where(lane == 0, beyond, roll(high, stride, 2))
            self.t[2, 1, line] = jnp.where(lane == 128 - stride, beyond, roll(low, 128 - stride, 2))
        for axis in range(3):
            self.merge(axis)
        for i in range(4):
            for j in range(4):
                add = neighbours(self.f, i, j) + weigh(self.f[0, i % 2, j], i)
                self.x[i, j] += change[i, j] * KEEP + self.g[i, j] * add


class Link:
    def __init__(self, px, qx, py, qy, pz, qz, send, recv, at):
        self.px, self.qx, self.py, self.qy, self.pz, self.qz = (px, qx, py, qy, pz, qz)
        gx, gy, gz = at

        def copy(src, dst, spot, device):
            return pltpu.make_async_remote_copy(
                src_ref=src,
                dst_ref=dst,
                send_sem=send.at[spot],
                recv_sem=recv.at[spot],
                device_id=device,
                device_id_type=MESH,
            )

        self.x_copies = [
            copy(px.at[0], qx.at[0], 0, {"gx": lax.rem(gx + 1, 32)}),
            copy(px.at[1], qx.at[1], 1, {"gx": lax.rem(gx + 31, 32)}),
        ]
        self.z_copies = [
            copy(pz.at[0], qz.at[0], 2, {"gz": lax.rem(gz + 1, 4)}),
            copy(pz.at[1], qz.at[1], 3, {"gz": lax.rem(gz + 3, 4)}),
        ]
        self.y_copies = [copy(py, qy, 4, {"gy": 1 - gy})]

    def start_x(self):
        for item in self.x_copies:
            item.start()

    def start_y(self):
        for item in self.y_copies:
            item.start()

    def start_z(self):
        for item in self.z_copies:
            item.start()

    def wait_x(self):
        for item in self.x_copies:
            item.wait_recv()

    def wait_y(self):
        for item in self.y_copies:
            item.wait_recv()

    def wait_z(self):
        for item in self.z_copies:
            item.wait_recv()

    def close(self):
        for item in self.x_copies + self.y_copies + self.z_copies:
            item.wait_send()


class Whole:
    def __init__(self, level, count, x, b, g, d, r, f, coefficient):
        self.level, self.count = (level, count)
        self.x, self.b, self.g, self.d, self.r, self.f = (x, b, g, d, r, f)
        self.coefficient = coefficient

    def faces(self):
        count = self.count
        ends = iota((count, 8, 128), 2) % 64
        value = self.coefficient[...]
        factors = [
            (value * (TAU * wide * SQ[0]), value * (TAU * wide * SQ[1]))
            for wide in level_scales(self.level)[:3]
        ]
        for first in range(4):
            for second in range(4):
                low, high = face_pair2(self.x, 0, first, second)
                before, after = (roll(high[count - 1 :], 1, 1), roll(low[:1], 7, 1))
                if count > 1:
                    before = jnp.concatenate([before, high[: count - 1]], axis=0)
                    after = jnp.concatenate([low[1:], after], axis=0)
                even, odd = factors[0]
                self.f[0, 0, first, second] = even * (before + after)
                self.f[0, 1, first, second] = odd * (before - after)
                low, high = face_pair2(self.x, 1, first, second)
                even, odd = factors[1]
                self.f[1, 0, first, second] = even * roll(high + low, 64, 2)
                self.f[1, 1, first, second] = odd * roll(high - low, 64, 2)
                low, high = face_pair2(self.x, 2, first, second)
                even, odd = factors[2]
                before = jnp.where(ends < 4, roll(high, 69, 2), roll(high, 4, 2))
                after = jnp.where(ends >= 60, roll(low, 59, 2), roll(low, 124, 2))
                self.f[2, 0, first, second] = even * (before + after)
                self.f[2, 1, first, second] = odd * (before - after)

    def tables(self):
        inverse_tables(self.g, self.d, self.coefficient[...], self.level)

    def before(self):
        first_guess(self.x, self.b, self.g)
        self.faces()
        sweep(self.x, self.b, self.g, self.f)

    def down(self, coarse):
        self.faces()
        residual(self.r, self.x, self.b, self.d, self.f)
        for j in range(4):
            for block in range(coarse.count):
                first = [self.r[i, j, :, 2 * block] for i in range(4)]
                second = [self.r[i, j, :, 2 * block + 1] for i in range(4)]
                for i, value in enumerate(restrict4(first, second)):
                    coarse.b[i, j, :, block] = value

    def up(self, coarse):
        for j in range(4):
            for block in range(coarse.count):
                low, high = extend4_pair([coarse.x[i, j, :, block] for i in range(4)])
                for i in range(4):
                    self.x[i, j, :, 2 * block] += low[i]
                    self.x[i, j, :, 2 * block + 1] += high[i]
        for step in range(2):
            self.faces()
            sweep(self.x, self.b, self.g, self.f)


class Beyond:
    def __init__(self, e, g, f, h, coefficient):
        self.e, self.g, self.f, self.h, self.coefficient = (e, g, f, h, coefficient)

    def smooth(self, count, beyond):
        value = self.coefficient[:count] * (TAU * level_scales(1)[0])
        even, odd = (value * SQ[0], value * SQ[1])
        low_rows = iota((8, 128), 0) < 4
        row, lane = (iota((count, 8, 128), 1) % 4, iota((count, 8, 128), 2))
        for first in range(4):
            for second in range(4):
                low, high = face_pair2(self.e, 0, first, second)
                ha, hb, hc = (high[block] for block in range(3))
                la, lb, lc = (low[block] for block in range(3))
                far = self.h[first, second] if beyond else hc
                ta, sa = (roll(ha, 4, 0), roll(la, 4, 0))
                before = [
                    jnp.where(low_rows, roll(hb, 4, 0), ta), jnp.where(low_rows, ta, hc), jnp.where(low_rows, hb, far)
                ]
                after = [
                    jnp.where(low_rows, sa, roll(lb, 4, 0)), jnp.where(low_rows, lc, sa), jnp.where(low_rows, far, lb)
                ]
                before, after = (jnp.stack(before[:count], axis=0), jnp.stack(after[:count], axis=0))
                self.f[0, 0, first, second, :count] = even * (before + after)
                self.f[0, 1, first, second, :count] = odd * (before - after)
                low, high = face_pair2(self.e, 1, first, second)
                low, high = (low[:count], high[:count])
                before = jnp.where(row == 0, roll(high, 5, 1), roll(high, 1, 1))
                after = jnp.where(row == 3, roll(low, 3, 1), roll(low, 7, 1))
                self.f[1, 0, first, second, :count] = even * (before + after)
                self.f[1, 1, first, second, :count] = odd * (before - after)
                low, high = face_pair2(self.e, 2, first, second)
                low, high = (low[:count], high[:count])
                before = jnp.where(
                    lane == 0, roll(high, 1, 2), jnp.where(lane == 1, roll(high, 3, 2), roll(high, 2, 2))
                )
                after = jnp.where(
                    lane == 126, roll(low, 125, 2), jnp.where(lane == 127, roll(low, 127, 2), roll(low, 126, 2))
                )
                self.f[2, 0, first, second, :count] = even * (before + after)
                self.f[2, 1, first, second, :count] = odd * (before - after)
        for i in range(4):
            for j in range(4):
                for k in range(4):
                    add = weigh(self.f[0, i % 2, j, k, :count], i) + weigh(self.f[1, j % 2, i, k, :count], j)
                    add = add + weigh(self.f[2, k % 2, i, j, :count], k)
                    self.e[i, j, k, :count] = self.e[i, j, k, :count] * KEEP + self.g[i, j, k, :count] * add


def kernel(
    source_in,
    coefficient_in,
    orientation_in,
    out,
    source, coefficient, orientation, input_sem, output_sem,
    x0, b0, g0, d0, r0, t0, f0, signs,
    x1, b1, g1, d1, r1, t1, f1, c1, w1, v1,
    x2, b2, g2, d2, r2, f2, c2,
    x3, b3, g3, d3, r3, f3, c3,
    x4, b4, g4, d4, r4, f4, c4,
    px, qx, py0, qy0, pz0, qz0, py1, qy1, pz1, qz1,
    cs, call, cline, cplane, cown, cin,
    ms, mall, my, mz,
    face_send, face_recv,
    c_send, c_recv, c_send2, c_recv2,
    m_send, m_recv, m_send2, m_recv2,
    told,
    e1, ge, fe, he, ce, de, halo1, halo0, wb,
    near_y, near_z, near_x, near_send, near_recv, spare,
):
    inputs = [
        pltpu.make_async_copy(src, dst, input_sem.at[spot])
        for spot, (src, dst) in enumerate(
            ((coefficient_in, coefficient), (source_in, source), (orientation_in, orientation))
        )
    ]
    for item in inputs:
        item.start()
    gx, gy, gz = (lax.axis_index("gx"), lax.axis_index("gy"), lax.axis_index("gz"))
    slow, fast = (gx // 4, lax.rem(gx, 4))
    slow_at = pl.multiple_of(slow * 16, 16)
    slow_at8 = pl.multiple_of(slow * 8, 8)
    nearest = (0, 1, 7, 2, 6, 3, 5, 4)
    offsets = [(a, b) for a in nearest for b in range(4) if (a, b) != (0, 0)]

    def along_x(a, b):
        return {"gx": lax.rem(slow + a, 8) * 4 + lax.rem(fast + b, 4)}

    def beside(step):
        return {"gx": lax.rem(gx + step + 32, 32)}

    up_z, down_z = (lax.rem(gz + 1, 4), lax.rem(gz + 3, 4))
    around = [
        {"gy": 1 - gy},
        {"gz": up_z},
        {"gy": 1 - gy, "gz": up_z},
        {"gz": down_z},
        {"gy": 1 - gy, "gz": down_z},
    ]

    barrier = pltpu.get_barrier_semaphore()
    for device in (beside(1), beside(-1), {"gy": 1 - gy}, {"gz": up_z}, {"gz": down_z}):
        pl.semaphore_signal(barrier, inc=1, device_id=device, device_id_type=MESH)

    for item in inputs:
        item.wait()
    for i in range(4):
        for k, value in enumerate(into_modes(*[source[i, :, k] for k in range(4)])):
            b0[i, :, k] = value
    for i in range(4):
        for j, value in enumerate(into_modes(*[b0[i, j] for j in range(4)])):
            b0[i, j] = value
    for j in range(4):
        for i, value in enumerate(into_modes(*[b0[i, j] for i in range(4)])):
            b0[i, j] = value
    inverse_tables(g0, d0, coefficient[...], 0)
    first_guess(x0, b0, g0)
    for face in range(6):
        code = orientation[face]
        one = jnp.ones((16, 128), F32)
        first = jnp.where(code // 2 % 2 == 1, -one, one)
        second = jnp.where(code // 4 == 1, -one, one)
        signs[face, 0] = jnp.stack([one, second, one, second], axis=0)
        signs[face, 1] = jnp.stack([first, first * second, first, first * second], axis=0)

    row8 = iota((8, 128), 0)
    lane8 = iota((8, 128), 1)
    top, bottom = (coefficient[:8], coefficient[8:])
    value = 0.5 * (
        jnp.where(row8 < 4, top, roll(bottom, 4, 0)) + jnp.where(row8 < 4, roll(top, 4, 0), bottom)
    )
    value = 0.5 * (value + roll(value, 7, 0))
    value = 0.5 * (value + roll(value, 127, 1))
    c1[...] = value
    inverse_tables(g1, d1, value, 1)
    value = 0.5 * (value + roll(value, 4, 0))
    value = 0.5 * (value + roll(value, 6, 0))
    cs[...] = 0.5 * (value + roll(value, 126, 1))

    pl.semaphore_wait(barrier, 5)

    def tell(step):
        devices = [beside(2**step), beside(-(2**step))]
        if step == 0:
            devices.append({"gy": 1 - gy})
        for device in devices:
            pl.semaphore_signal(told.at[step], inc=1, device_id=device, device_id_type=MESH)

    def heard(step):
        pl.semaphore_wait(told.at[step], 3 if step == 0 else 2)
        if step < 3:
            tell(step + 1)

    def link(level, step):
        spot = 4 * level + step
        py, qy, pz, qz = (py0, qy0, pz0, qz0) if level == 0 else (py1, qy1, pz1, qz1)
        return Link(
            px.at[spot], qx.at[spot], py.at[step], qy.at[step], pz.at[step], qz.at[step],
            face_send.at[spot], face_recv.at[spot], (gx, gy, gz),
        )

    def copy(src, dst, send, recv, device):
        return pltpu.make_async_remote_copy(
            src_ref=src, dst_ref=dst, send_sem=send, recv_sem=recv, device_id=device, device_id_type=MESH
        )

    fine = Halo(16, 1, x0, b0, g0, d0, r0, t0, f0, coefficient, 1.0, orientation, signs)
    mid = Halo(8, 2, x1, b1, g1, d1, r1, t1, f1, c1, 2.0, None, None)
    links = []

    c_line = [copy(cs, call.at[fast], c_send.at[0, b], c_recv.at[0, b], along_x(0, b)) for b in range(1, 4)]
    c_copies = [
        copy(cline, cplane.at[pl.ds(slow_at8, 8)], c_send.at[a, 0], c_recv.at[a, 0], along_x(a, 0))
        for a in nearest[1:]
    ]

    def send_line():
        for item in c_line:
            item.start()

    near_copies = [copy(c1, near_y, near_send.at[0], near_recv.at[0], {"gy": 1 - gy})]
    ring = iota((8, 128), 0) % 4

    def near_step(step):
        if step == 0:
            near_copies[0].wait_recv()
            own, other = (c1[...], near_y[...])
            value = jnp.where(ring < 2, jnp.where(ring == 0, own, roll(own, 7, 0)),
                              jnp.where(ring == 2, roll(other, 2, 0), roll(other, 1, 0)))
            spare[0] = value
            for spot, device in ((1, {"gz": down_z}), (2, {"gz": up_z})):
                item = copy(spare.at[0], near_z.at[spot - 1], near_send.at[spot], near_recv.at[spot], device)
                item.start()
                near_copies.append(item)
        elif step == 1:
            near_copies[1].wait_recv()
            near_copies[2].wait_recv()
            outer = jnp.where(lane8 < 64, roll(near_z[0], 1, 1), roll(near_z[1], 1, 1))
            value = jnp.where(lane8 % 2 == 0, spare[0], outer)
            spare[1] = value
            ce[0] = value
            for spot, device in ((3, beside(-1)), (4, beside(1))):
                item = copy(spare.at[1], near_x.at[spot - 3], near_send.at[spot], near_recv.at[spot], device)
                item.start()
                near_copies.append(item)
        else:
            near_copies[3].wait_recv()
            near_copies[4].wait_recv()
            after, before = (near_x[0], near_x[1])
            ce[1] = jnp.where(row8 < 4, after, before)
            ce[2] = jnp.where(row8 < 4, roll(after, 4, 0), roll(before, 4, 0))
            inverse_tables(ge, de, ce[...], 1)

    links.append(link(0, 0))
    fine.send(links[-1], lambda: tell(0))
    near_copies[0].start()
    fine.receive(links[-1], False, lambda: near_step(0))
    heard(0)
    links.append(link(0, 1))
    fine.send(links[-1])
    fine.receive(links[-1], True, lambda: near_step(1))
    row4 = iota((4, 8, 128), 1)
    lane4 = iota((4, 8, 128), 2)
    for j in range(4):
        first, second = ([], [])
        for i in range(4):
            top, bottom = (r0[i, j, :, :8], r0[i, j, :, 8:])
            first.append(jnp.where(row4 < 4, top, roll(bottom, 4, 1)))
            second.append(jnp.where(row4 < 4, roll(top, 4, 1), bottom))
        for i, value in enumerate(restrict4(first, second)):
            w1[i, j] = value
    for i in range(4):
        first = [w1[i, j] for j in range(4)]
        for j, value in enumerate(restrict4(first, [roll(item, 7, 1) for item in first])):
            v1[i, j] = value
    for i in range(4):
        first = [v1[i, :, k] for k in range(4)]
        for k, value in enumerate(restrict4(first, [roll(item, 127, 2) for item in first])):
            b1[i, :, k] = value

    first_guess(x1, b1, g1)
    links.append(link(1, 0))
    mid.send(links[-1], lambda: (heard(1), send_line()))
    mid.receive(links[-1], False, lambda: (heard(2), near_step(2)))
    links.append(link(1, 1))
    mid.send(links[-1])
    def send_coefficients():
        heard(3)
        for item in c_line:
            item.wait_recv()
        call[fast] = cs[...]
        lines = [jnp.broadcast_to(call[block, pl.ds(0, 1), :], (8, 128)) for block in range(4)]
        cline[...] = jnp.where(row8 < 2, jnp.where(row8 == 0, lines[0], lines[1]),
                               jnp.where(row8 == 2, lines[2], lines[3]))
        for item in c_copies:
            item.start()
        cplane[pl.ds(slow_at8, 8), :] = cline[...]

    mid.receive(links[-1], True, send_coefficients)
    for j in range(4):
        first = [r1[i, j] for i in range(4)]
        for i, value in enumerate(restrict4(first, [roll(item, 4, 1) for item in first])):
            w1[i, j] = value
    for i in range(4):
        first = [w1[i, j] for j in range(4)]
        for j, value in enumerate(restrict4(first, [roll(item, 6, 1) for item in first])):
            v1[i, j] = value
    packed = []
    for i in range(4):
        first = [v1[i, :, k] for k in range(4)]
        total = None
        for k, value in enumerate(restrict4(first, [roll(item, 126, 2) for item in first])):
            total = value if k == 0 else jnp.where(lane4 % 4 == k, roll(value, k, 2), total)
        packed += [total[j] for j in range(4)]
    for line in range(8):
        low, high = (packed[line], packed[line + 8])
        ms[pl.ds(line, 1), :] = jnp.where(lane8 < 64, low, roll(high, 64, 1))[:1]
        ms[pl.ds(line + 8, 1), :] = jnp.where(lane8 < 64, roll(low, 64, 1), high)[:1]

    m_copies = {
        (a, b): copy(ms, mall.at[fast, pl.ds(slow_at, 16)], m_send.at[a, b], m_recv.at[a, b], along_x(a, b))
        for a, b in offsets
    }
    for item in m_copies.values():
        item.start()
    mall[fast, pl.ds(slow_at, 16), :] = ms[...]
    for item in c_copies:
        item.wait_recv()
    for block in range(4):
        cown[block] = cplane[pl.ds(block, 8, stride=8), :]
    c_around = [
        copy(cown, cin.at[spot], c_send2.at[spot], c_recv2.at[spot], device)
        for spot, device in enumerate(around)
    ]
    for item in c_around:
        item.start()
    for i in range(4):
        for j in range(4):
            x1[i, j] += g1[i, j] * r1[i, j]
    links.append(link(1, 2))
    mid.send(links[-1])
    passed = []
    for a in nearest:
        for b in range(4):
            if (a, b) != (0, 0):
                m_copies[a, b].wait_recv()
        start = lax.rem(slow + 8 - a, 8)
        start16 = pl.multiple_of(start * 16, 16)
        start8 = pl.multiple_of(start * 8, 8)
        upper = pl.multiple_of(start * 16 + 8, 8)
        for spot, device in enumerate(around):
            if spot == 0:
                src, dst = (mall.at[:, pl.ds(start16, 16)], my.at[:, pl.ds(start16, 16)])
            else:
                src = mall.at[:, pl.ds(upper if spot < 3 else start16, 8)]
                dst = mz.at[spot - 1, :, pl.ds(start8, 8)]
            item = copy(src, dst, m_send2.at[spot, a], m_recv2.at[spot, a], device)
            item.start()
            passed.append(item)
    for item in c_around:
        item.wait_recv()
    for block in range(4):
        mine, other = (cown[block], cin[0, block])
        below, below_other, above, above_other = (cin[spot, block] for spot in range(1, 5))
        phase = lane8 % 4
        near = jnp.where(phase == 0, roll(below, 64, 1), roll(mine, 1, 1))
        near = jnp.where(phase == 2, roll(mine, 66, 1), near)
        near = jnp.where(phase == 3, roll(above, 3, 1), near)
        far = jnp.where(phase == 0, below_other, roll(other, 65, 1))
        far = jnp.where(phase == 2, roll(other, 2, 1), far)
        far = jnp.where(phase == 3, roll(above_other, 67, 1), far)
        c2[block] = jnp.where(lane8 < 64, near, far)
    for block in range(2):
        c3[block] = 0.5 * (c2[2 * block] + c2[2 * block + 1])
    c4[0] = 0.5 * (c3[0] + c3[1])
    level2 = Whole(2, 4, x2, b2, g2, d2, r2, f2, c2)
    level3 = Whole(3, 2, x3, b3, g3, d3, r3, f3, c3)
    level4 = Whole(4, 1, x4, b4, g4, d4, r4, f4, c4)
    for level in (level2, level3, level4):
        level.tables()
    mid.receive(links[-1], False)
    links.append(link(1, 3))
    mid.send(links[-1])
    for i in range(4):
        for j in range(4):
            x0[i, j] += g0[i, j] * r0[i, j]
    for item in passed:
        item.wait_recv()

    def unpack(block, carry):
        odd, pair = (lane8 % 2 == 1, lane8 % 4 >= 2)
        for line in range(8):
            def rows(ref, start, stride):
                return ref[block, pl.ds(start, 8, stride=stride), :]

            near = [
                rows(mz.at[0], line, 8), rows(mall, line, 16), rows(mall, line + 8, 16), rows(mz.at[2], line, 8)
            ]
            far = [
                rows(mz.at[1], line, 8), rows(my, line, 16), rows(my, line + 8, 16), rows(mz.at[3], line, 8)
            ]
            for half in range(2):
                if half == 0:
                    part = [jnp.where(lane8 < 64, a, roll(b, 64, 1)) for a, b in zip(near, far)]
                else:
                    part = [jnp.where(lane8 < 64, roll(a, 64, 1), b) for a, b in zip(near, far)]
                step = [
                    jnp.where(odd, roll(part[1], 1, 1), part[0]),
                    jnp.where(odd, part[1], roll(part[0], 127, 1)),
                    jnp.where(odd, roll(part[3], 1, 1), part[2]),
                    jnp.where(odd, part[3], roll(part[2], 127, 1)),
                ]
                last = [
                    jnp.where(pair, roll(step[2], 2, 1), step[0]),
                    jnp.where(pair, roll(step[3], 2, 1), step[1]),
                    jnp.where(pair, step[2], roll(step[0], 126, 1)),
                    jnp.where(pair, step[3], roll(step[1], 126, 1)),
                ]
                mode = line + 8 * half
                for k in range(4):
                    b2[mode // 4, mode % 4, k, block] = last[k]
        return carry

    lax.fori_loop(0, 4, unpack, 0)
    level2.before()
    level2.down(level3)
    level3.before()
    level3.down(level4)
    level4.before()
    level3.up(level4)
    level2.up(level3)

    def element(step):
        place = lax.rem(gx + step + 32, 32)
        return place // 4, lax.rem(place, 4)

    def take(i, j, step):
        at, block = element(step)
        return jnp.broadcast_to(x2[i, j, :, block, pl.ds(at, 1), :], (4, 8, 128))

    def spread(value):
        value = jnp.where(row4 % 4 < 2, value, roll(value, 64, 2))
        low = jnp.where(lane4 % 2 == 0, roll(value, 127, 2), roll(value, 126, 2))
        high = jnp.where(lane4 % 2 == 0, roll(value, 62, 2), roll(value, 65, 2))
        value = jnp.where(lane4 < 64, low, high)
        return jnp.where(lane4 % 4 < 2, value, roll(value, 2, 2))

    one = jnp.ones((4, 8, 128), F32)
    sign_z = jnp.where(lane4 % 4 < 2, one, -one)
    sign_y = jnp.where(row4 % 2 == 0, one, -one)
    sign_x = jnp.where(row4 < 4, one, -one)
    for i in range(4):
        for j in range(4):
            w1[i, j] = spread(take(i, j, 0))
            wb[i, j] = spread(jnp.where(row4 < 4, take(i, j, 1), take(i, j, -1)))
    for j in range(4):
        after = [take(i, j, 2) for i in range(4)]
        before = [take(i, j, -2) for i in range(4)]
        low = (after[0] + after[2]) + (after[1] + after[3])
        high = (before[0] + before[2]) - (before[1] + before[3])
        he[j] = spread(jnp.where(row4 < 4, low, high))
    for ref in (w1, wb):
        for i in range(4):
            for k, value in enumerate(extend4([ref[i, :, k] for k in range(4)], sign_z)):
                ref[i, :, k] = value
        for i in range(4):
            for j, value in enumerate(extend4([ref[i, j] for j in range(4)], sign_y)):
                ref[i, j] = value
    for k, value in enumerate(extend4([he[:, k] for k in range(4)], sign_z)):
        he[:, k] = value
    for j, value in enumerate(extend4([he[j] for j in range(4)], sign_y)):
        he[j] = value
    for j in range(4):
        for i, value in enumerate(extend4([w1[i, j] for i in range(4)], sign_x)):
            e1[i, j, :, 0] = value
        for i, (value, other) in enumerate(zip(*extend4_mirrored([wb[i, j] for i in range(4)], sign_x))):
            e1[i, j, :, 1] = value
            e1[i, j, :, 2] = other
    beyond = Beyond(e1, ge, fe, he, ce)
    beyond.smooth(3, True)
    beyond.smooth(2, False)

    mid.land_y(links[-1])
    mid.land_z(links[-1])
    mid.land_x(links[-1])

    def own_rows(value):
        return jnp.where(row4 % 4 == 2, roll(value, 1, 1), value)

    for line in range(4):
        parts = [e1[i, line, :, 1] for i in range(4)]
        even, odd = (parts[0] + parts[2], parts[1] + parts[3])
        value = own_rows(roll(jnp.where(row4 < 4, even + odd, even - odd), 4, 1))
        halo1[0, line] = value + jnp.where(row4 < 4, t1[0, 0, line], t1[0, 1, line])
        parts = [e1[line, j, :, 0] for j in range(4)]
        even, odd = (parts[0] + parts[2], parts[1] + parts[3])
        value = jnp.where(row4 % 4 == 0, roll(even - odd, 5, 1), even + odd)
        halo1[1, line] = value + jnp.where(row4 % 4 == 0, t1[1, 0, line], t1[1, 1, line])
        parts = [e1[line, :, k, 0] for k in range(4)]
        even, odd = (parts[0] + parts[2], parts[1] + parts[3])
        value = own_rows(jnp.where(lane4 < 64, roll(even - odd, 1, 2), roll(even + odd, 125, 2)))
        halo1[2, line] = value + jnp.where(lane4 < 64, t1[2, 0, line], t1[2, 1, line])

    def fill(value):
        value = jnp.where(row4 % 2 == 0, value, roll(value, 1, 1))
        return jnp.where(lane4 % 2 == 0, value, roll(value, 1, 2))

    def doubled(value):
        turned = roll(value, 4, 1)
        low, high = (jnp.where(row4 < 4, value, turned), jnp.where(row4 < 4, turned, value))
        return jnp.concatenate([low, high], axis=1)

    for i in range(4):
        for j in range(4):
            w1[i, j] = fill(x1[i, j] + own_rows(e1[i, j, :, 0]))
    for axis in range(3):
        for line in range(4):
            halo1[axis, line] = fill(halo1[axis, line])
    sign_z = jnp.where(lane4 % 2 == 0, one, -one)
    wide_one = jnp.ones((4, 16, 128), F32)
    sign_x = jnp.where(iota((4, 16, 128), 1) % 8 < 4, wide_one, -wide_one)
    for i in range(4):
        for k, value in enumerate(extend4([w1[i, :, k] for k in range(4)], sign_z)):
            w1[i, :, k] = value
    for i in range(4):
        for j, value in enumerate(extend4([w1[i, j] for j in range(4)], sign_y)):
            w1[i, j] = value
    for j in range(4):
        for i, value in enumerate(extend4([doubled(w1[i, j]) for i in range(4)], sign_x)):
            r0[i, j] = value
    for axis in range(2):
        for k, value in enumerate(extend4([halo1[axis, :, k] for k in range(4)], sign_z)):
            halo1[axis, :, k] = value
    for line, value in enumerate(extend4([halo1[0, line] for line in range(4)], sign_y)):
        halo0[0, line, :, :8] = value
    for line, value in enumerate(extend4([doubled(halo1[1, line]) for line in range(4)], sign_x)):
        halo0[1, line] = value
    for line, value in enumerate(extend4([halo1[2, :, line] for line in range(4)], sign_y)):
        halo1[2, :, line] = value
    for line, value in enumerate(extend4([doubled(halo1[2, line]) for line in range(4)], sign_x)):
        halo0[2, line] = value
    fine.correct(r0, halo0)
    links.append(link(0, 2))
    fine.send(links[-1])
    fine.receive(links[-1], False)

    for j in range(4):
        for i, value in enumerate(from_modes(*[x0[i, j] for i in range(4)])):
            x0[i, j] = value
    outputs = []
    for i in range(4):
        for k, value in enumerate(from_modes(*[x0[i, :, k] for k in range(4)])):
            x0[i, :, k] = value
        for j, value in enumerate(from_modes(*[x0[i, j] for j in range(4)])):
            x0[i, j] = value
        outputs.append(pltpu.make_async_copy(x0.at[i], out.at[i], output_sem.at[i]))
        outputs[-1].start()
    for item in links:
        item.close()
    for item in outputs:
        item.wait()
    for item in near_copies + c_line + c_copies + c_around + list(m_copies.values()) + passed:
        item.wait_send()


def scratch():
    def mem(*shape):
        return pltpu.VMEM(shape, F32)

    modes = (4, 4, 4)
    dma = pltpu.SemaphoreType.DMA
    inputs = [mem(*modes, 16, 128), mem(16, 128), pltpu.VMEM((6, 16, 128), jnp.int32), dma((3,)), dma((4,))]
    level0 = [mem(*modes, 16, 128)] * 5 + [
        mem(3, 2, 4, 4, 16, 128), mem(3, 2, 4, 4, 16, 128), mem(6, 2, 4, 16, 128)
    ]
    level1 = [mem(*modes, 8, 128)] * 5 + [
        mem(3, 2, 4, 4, 8, 128), mem(3, 2, 4, 4, 8, 128), mem(8, 128), mem(*modes, 8, 128), mem(*modes, 8, 128)
    ]
    whole = []
    for count in (4, 2, 1):
        whole += [mem(*modes, count, 8, 128)] * 5 + [mem(3, 2, 4, 4, count, 8, 128), mem(count, 8, 128)]
    faces = [
        mem(8, 2, 2, 4, 8, 128), mem(8, 2, 2, 4, 8, 128),
        mem(4, 2, 4, 4, 16, 128), mem(4, 2, 4, 4, 16, 128), mem(4, 2, 16, 128), mem(4, 2, 16, 128),
        mem(4, 2, 4, 4, 8, 128), mem(4, 2, 4, 4, 8, 128), mem(4, 2, 8, 128), mem(4, 2, 8, 128),
    ]
    gathered = [
        mem(8, 128), mem(4, 8, 128), mem(8, 128), mem(64, 128), mem(4, 8, 128), mem(5, 4, 8, 128),
        mem(16, 128), mem(4, 128, 128), mem(4, 128, 128), mem(4, 4, 64, 128),
    ]
    sems = [dma((8, 5)), dma((8, 5)), dma((8, 4)), dma((8, 4)), dma((5,)), dma((5,)),
            dma((8, 4)), dma((8, 4)), dma((5, 8)), dma((5, 8)),
            pltpu.SemaphoreType.REGULAR((4,))]
    extended = [
        mem(*modes, 3, 8, 128), mem(*modes, 3, 8, 128), mem(3, 2, 4, 4, 3, 8, 128), mem(4, 4, 8, 128),
        mem(3, 8, 128), mem(*modes, 3, 8, 128), mem(3, 4, 4, 8, 128), mem(3, 4, 4, 16, 128), mem(*modes, 8, 128),
        mem(8, 128), mem(2, 8, 128), mem(2, 8, 128), dma((5,)), dma((5,)), mem(2, 8, 128),
    ]
    return inputs + level0 + level1 + whole + faces + gathered + sems + extended


def local(source, coefficient, orientation):
    out = pl.pallas_call(
        kernel,
        out_shape=jax.ShapeDtypeStruct((4, 4, 4, 16, 128), F32),
        in_specs=[pl.BlockSpec(memory_space=pl.ANY)] * 3,
        out_specs=pl.BlockSpec(memory_space=pl.ANY),
        scratch_shapes=scratch(),
        compiler_params=pltpu.CompilerParams(
            collective_id=0, has_side_effects=True, vmem_limit_bytes=64 * 1024 * 1024 - 65536
        ),
    )(
        source.reshape(4, 4, 4, 16, 128),
        coefficient.reshape(16, 128),
        orientation.reshape(6, 16, 128),
    )
    return out.reshape(4, 4, 4, 4, 4, 128)


def solution(mesh):
    in_specs = (
        P(None, None, None, "gx", "gy", "gz"),
        P("gx", "gy", "gz"),
        P(None, "gx", "gy", "gz"),
    )
    out_specs = P(None, None, None, "gx", "gy", "gz")
    return jax.shard_map(local, mesh=mesh, in_specs=in_specs, out_specs=out_specs, check_vma=False)
```
